256 devices in a mesh: section: 16 (over y_lo, z), expert: 16 (over x, y_hi, core).
Axes of the slice: x: 4, y: 4 (y_hi: 2, y_lo: 2; y = y_hi * 2 + y_lo), z: 8, core: 2. Of those that a mesh axis runs over, the one named last changes fastest.
Arguments:
- carried: bfloat16 [16, 2048, 2048], P('section', 'expert'), may hold values from -6 to 6
- saved_rows: bfloat16 [16, 2048, 2048], P('section', 'expert'), may hold values from -6 to 6
- returned: bfloat16 [16, 2048, 2048], P('section', 'expert'), may hold values from -6 to 6
- fwd_ids: int32 [16, 2048, 2], P('section', 'expert'), may hold values from 0 to 3, all different within a row; in each aligned block of 128 rows (0 to 127, 128 to 255, ..., all dimensions but the last counted through in order) at most 72 rows name the same one
- fwd_gates: float32 [16, 2048, 2], P('section', 'expert'), may hold values from 0.2 to 1
- bwd_ids: int32 [16, 2048, 2], P('section', 'expert'), may hold values from 0 to 3, all different within a row; in each aligned block of 128 rows (0 to 127, 128 to 255, ..., all dimensions but the last counted through in order) at most 72 rows name the same one
- bwd_gates: float32 [16, 2048, 2], P('section', 'expert'), may hold values from 0.2 to 1
- gate_w: bfloat16 [16, 2048, 4096], P('section', None, 'expert'), may hold values from -0.125 to 0.125
- up_w: bfloat16 [16, 2048, 4096], P('section', None, 'expert'), may hold values from -0.125 to 0.125
- down_w: bfloat16 [16, 4096, 2048], P('section', 'expert'), may hold values from -0.1875 to 0.1875
Outputs:
- next_input: bfloat16 [16, 2048, 2048], P('section', 'expert')
- grad_input: bfloat16 [16, 2048, 2048], P('section', 'expert')
- gate_grad: float32 [16, 2048, 4096], P('section', None, 'expert')
- up_grad: float32 [16, 2048, 4096], P('section', None, 'expert')
- down_grad: float32 [16, 4096, 2048], P('section', 'expert')
The draws below stay inside these ranges and needn't reach their ends.
Inputs may be any that keep to these rules, and one draw needn't show every extreme that they name: `fwd_ids`: the 2 ids of a token differ. In each aligned block of 128 tokens (one device's tokens of one section) each expert is named by at most 72 tokens, a bound that some block reaches. `bwd_ids`: the 2 ids of a token differ. In each aligned block of 128 tokens each expert is named by at most 72 tokens, a bound that some block reaches.
All inputs are finite; a program needn't handle non-finite values.
Results may differ from the reference program's by a relative error of at most 0.0052.
Values may be sent and summed in bfloat16 or wider, within the bound.
A program may use at most 128 MiB of HBM per device.

```python
import math
import jax
import jax.numpy as jnp
import numpy as np
from jax import lax

D = 2048
H_WIN = 1024
E_WIN = 4
TOP = 2
TOK_DEV = 128
CAP = 72
SECTIONS = 16
TOKENS = 2048
N_EXPERT = 16


def block_scale(stream_key, shape, split, low, high):
    loudness, own = 1.0, jax.random.fold_in(stream_key, 6)
    for position, parts in split:
        steps = jnp.exp(jax.random.uniform(jax.random.fold_in(own, position), (parts,), jnp.float32, low / len(split), high / len(split)))
        loudness = loudness * jnp.repeat(steps, shape[position] // parts).reshape([-1 if axis == position else 1 for axis in range(len(shape))])
    return loudness


def assign_block(own_key, own, number, rows, number_of, top, reach, skew):
    ranking = jax.random.permutation(own_key, number_of)
    crowded, usual = shares(number_of, rows * top, reach, skew, True), shares(number_of, rows * top, reach, skew, False)
    places = jnp.arange(number_of)

    def named(sizes, offset_by):
        used = int((sizes > 0).sum())
        fixed = max(1, used // 4)
        passed = fixed + (places - fixed + offset_by * (used - fixed)) % max(1, number_of - fixed)
        return jnp.zeros((number_of,), jnp.int32).at[ranking[jnp.where(places < fixed, places, passed)]].set(jnp.asarray(sizes, jnp.int32))

    sizes = jnp.where(number % 4 == 0, named(crowded, number // 4), named(usual, number - number // 4 - 1))
    mixed = jax.random.permutation(jax.random.fold_in(own, 3), number_of)
    source_of, receiver = mixed[0:number_of // 2 * 2:2], mixed[1:number_of // 2 * 2:2]
    room = jnp.minimum(sizes[source_of] - 1, reach - sizes[receiver]) // 2
    room = jnp.where((source_of == ranking[0]) | (receiver == ranking[0]) | (sizes[receiver] == 0), 0, jnp.maximum(room, 0))
    passed = jax.random.randint(jax.random.fold_in(own, 4), (number_of // 2,), 0, 1 << 20) % (room + 1)
    sizes = sizes.at[source_of].add(-passed).at[receiver].add(passed)
    items = jnp.searchsorted(jnp.cumsum(sizes), jnp.arange(rows * top), side="right").astype(jnp.int32)
    listing = items.reshape(top, rows).T
    listing = listing[jax.random.permutation(jax.random.fold_in(own, 1), rows)]
    offset_by = jax.random.randint(jax.random.fold_in(own, 2), (rows, 1), 0, top)
    return jnp.take_along_axis(listing, (jnp.arange(top)[None, :] + offset_by) % top, axis=1)


def shares(count, total, reach, slope, full):
    loads = [(1 << 20) // math.isqrt(grade ** slope) + 1 for grade in range(1, count + 1)]
    largest = reach if full else min(reach, max(-(-total // count), total * loads[0] // sum(loads)))
    least = 1 if total - largest >= count - 1 else 0
    holding, rest = [largest] + [least] * (count - 1), total - largest - least * (count - 1)
    while rest > 0:
        movable = [i for i in range(1, count) if holding[i] < largest] or [i for i in range(1, count) if holding[i] < reach]
        mass, remaining = sum([loads[i] for i in movable]), rest
        for i in movable:
            more = min(reach - holding[i], max(1, remaining * loads[i] // mass), rest)
            holding[i] = holding[i] + more
            rest = rest - more
    return np.array(holding)


def scatter_about(key, shape, width, most, split=(), dtype=jnp.bfloat16):
    values = width * jax.random.normal(key, shape, jnp.float32)
    if split:
        values = values * block_scale(key, shape, split, -0.22, 0.18)
    return jnp.clip(values, -most, most).astype(dtype)


def setup_inputs(seed: int = 0) -> dict:
    splits = jax.random.split(jax.random.key(seed), 11)
    carried = scatter_about(splits[0], (SECTIONS, TOKENS, D), 1.0, 6.0, ((0, 16), (1, 16)))
    saved_rows = scatter_about(splits[1], (SECTIONS, TOKENS, D), 1.0, 6.0, ((0, 16), (1, 16)))
    returned = scatter_about(splits[2], (SECTIONS, TOKENS, D), 1.0, 6.0, ((0, 16), (1, 16)))
    fwd_ids_keys = jax.random.split(jax.random.fold_in(splits[3], 1), SECTIONS * TOKENS // TOK_DEV)
    fwd_ids_turns = jax.random.permutation(jax.random.fold_in(splits[3], 3), SECTIONS * TOKENS // TOK_DEV)
    fwd_ids = jax.vmap(lambda own, number: assign_block(jax.random.fold_in(splits[3], 2), own, number, TOK_DEV, E_WIN, TOP, CAP, 2))(fwd_ids_keys, fwd_ids_turns).reshape((SECTIONS, TOKENS, TOP))
    fwd_gates = jnp.clip(jnp.exp(math.log(1.0) - 1.609438 * jax.random.uniform(splits[4], (SECTIONS, TOKENS, TOP), jnp.float32) ** block_scale(splits[4], (SECTIONS, TOKENS, TOP), ((0, 16), (1, 16)), -0.2, 0.2)), 0.2, 1.0)
    bwd_ids_keys = jax.random.split(jax.random.fold_in(splits[5], 1), SECTIONS * TOKENS // TOK_DEV)
    bwd_ids_turns = jax.random.permutation(jax.random.fold_in(splits[5], 3), SECTIONS * TOKENS // TOK_DEV)
    bwd_ids = jax.vmap(lambda own, number: assign_block(jax.random.fold_in(splits[5], 2), own, number, TOK_DEV, E_WIN, TOP, CAP, 2))(bwd_ids_keys, bwd_ids_turns).reshape((SECTIONS, TOKENS, TOP))
    bwd_gates = jnp.clip(jnp.exp(math.log(1.0) - 1.609438 * jax.random.uniform(splits[6], (SECTIONS, TOKENS, TOP), jnp.float32) ** block_scale(splits[6], (SECTIONS, TOKENS, TOP), ((0, 16), (1, 16)), -0.2, 0.2)), 0.2, 1.0)
    gate_w = scatter_about(splits[7], (SECTIONS, D, E_WIN * H_WIN), D ** -0.5, 0.125, ((0, 16), (2, 16)))
    up_w = scatter_about(splits[8], (SECTIONS, D, E_WIN * H_WIN), D ** -0.5, 0.125, ((0, 16), (2, 16)))
    down_w = scatter_about(splits[9], (SECTIONS, E_WIN * H_WIN, D), H_WIN ** -0.5, 0.1875, ((0, 16), (1, 16)))
    return {"carried": carried, "saved_rows": saved_rows, "returned": returned, "fwd_ids": fwd_ids, "fwd_gates": fwd_gates, "bwd_ids": bwd_ids, "bwd_gates": bwd_gates, "gate_w": gate_w, "up_w": up_w, "down_w": down_w}


def expert_order(route_ids, route_gates, expert):
    hit = route_ids == expert
    share = jnp.sum(jnp.where(hit, route_gates, jnp.zeros_like(route_gates)), axis=1)
    chosen = jnp.any(hit, axis=1)
    keyed = jnp.where(chosen, 0, 1).astype(jnp.int32)
    order = jnp.argsort(keyed, stable=True)[: N_EXPERT * CAP].astype(jnp.int32)
    return order, share[order]


def section_pass(packed):
    layer_in, fwd_route, fwd_weight, saved_in, bwd_route, bwd_weight, cotangent, gate_mat, up_mat, down_mat = packed
    group_size = N_EXPERT // E_WIN
    slice_width = H_WIN // group_size
    output_sum = layer_in.astype(jnp.float32)
    input_grad = cotangent.astype(jnp.float32)
    gate_cols = []
    up_cols = []
    down_rows = []
    for expert in range(E_WIN):
        first = expert * H_WIN
        gate_part = gate_mat[:, first:first + H_WIN]
        up_part = up_mat[:, first:first + H_WIN]
        down_part = down_mat[first:first + H_WIN, :]
        order, share = expert_order(fwd_route, fwd_weight, expert)
        token_rows = layer_in[order]
        pre_gate = jnp.dot(token_rows, gate_part, preferred_element_type=jnp.float32)
        pre_up = jnp.dot(token_rows, up_part, preferred_element_type=jnp.float32)
        sigma = jax.nn.sigmoid(pre_gate)
        hidden = (pre_gate * sigma * pre_up).astype(jnp.bfloat16)
        expert_out = jnp.zeros((token_rows.shape[0], D), jnp.float32)
        for piece in range(group_size):
            low = piece * slice_width
            term = jnp.dot(hidden[:, low:low + slice_width], down_part[low:low + slice_width], preferred_element_type=jnp.float32).astype(jnp.bfloat16)
            expert_out = expert_out + lax.optimization_barrier(term).astype(jnp.float32)
        output_sum = output_sum.at[order].add(share[:, None] * expert_out)
        order_b, share_b = expert_order(bwd_route, bwd_weight, expert)
        saved = saved_in[order_b]
        scaled = (share_b[:, None] * cotangent[order_b].astype(jnp.float32)).astype(jnp.bfloat16)
        pre_gate2 = jnp.dot(saved, gate_part, preferred_element_type=jnp.float32)
        pre_up2 = jnp.dot(saved, up_part, preferred_element_type=jnp.float32)
        sigma2 = jax.nn.sigmoid(pre_gate2)
        swish = pre_gate2 * sigma2
        hidden2 = (swish * pre_up2).astype(jnp.bfloat16)
        grad_hidden = jnp.dot(scaled, down_part.T, preferred_element_type=jnp.float32)
        grad_gate_pre = (grad_hidden * pre_up2 * sigma2 * (1.0 + pre_gate2 * (1.0 - sigma2))).astype(jnp.bfloat16)
        grad_up_pre = (grad_hidden * swish).astype(jnp.bfloat16)
        back_sum = jnp.zeros((saved.shape[0], D), jnp.float32)
        for piece in range(group_size):
            low = piece * slice_width
            high = low + slice_width
            term = jnp.dot(grad_gate_pre[:, low:high], gate_part[:, low:high].T, preferred_element_type=jnp.float32)
            term = term + jnp.dot(grad_up_pre[:, low:high], up_part[:, low:high].T, preferred_element_type=jnp.float32)
            term = term.astype(jnp.bfloat16)
            back_sum = back_sum + lax.optimization_barrier(term).astype(jnp.float32)
        input_grad = input_grad.at[order_b].add(back_sum)
        gate_cols.append(jnp.dot(saved.T, grad_gate_pre, preferred_element_type=jnp.float32))
        up_cols.append(jnp.dot(saved.T, grad_up_pre, preferred_element_type=jnp.float32))
        down_rows.append(jnp.dot(hidden2.T, scaled, preferred_element_type=jnp.float32))
    return (output_sum.astype(jnp.bfloat16), input_grad.astype(jnp.bfloat16), jnp.concatenate(gate_cols, axis=1), jnp.concatenate(up_cols, axis=1), jnp.concatenate(down_rows, axis=0))


def reference(carried, saved_rows, returned, fwd_ids, fwd_gates, bwd_ids, bwd_gates, gate_w, up_w, down_w):
    arrived = jnp.roll(carried, 1, axis=0)
    incoming = jnp.roll(returned, -1, axis=0)
    results = lax.map(section_pass, (arrived, fwd_ids, fwd_gates, saved_rows, bwd_ids, bwd_gates, incoming, gate_w, up_w, down_w))
    return (results[0], results[1], results[2], results[3], results[4])
```

```python
import jax
import jax.numpy as jnp
from jax import lax
from jax.sharding import PartitionSpec as P

E_WIN = 4
CAP = 72


def passed_along(value, axis, steps):
    count = lax.axis_size(axis)
    pairs = [(source, (source + steps) % count) for source in range(count)]
    return lax.ppermute(value, axis, pairs)


def slot_table(route_ids):
    flat = route_ids.reshape(-1)
    onehot = (flat[:, None] == jnp.arange(E_WIN, dtype=jnp.int32)[None, :]).astype(jnp.int32)
    rows = flat.shape[0]
    earlier = (jnp.arange(rows)[:, None] > jnp.arange(rows)[None, :]).astype(jnp.bfloat16)
    before = jnp.dot(earlier, onehot.astype(jnp.bfloat16), preferred_element_type=jnp.float32).astype(jnp.int32)
    ranking = jnp.sum(before * onehot, axis=1)
    return (flat * CAP + ranking).reshape(route_ids.shape)


def spread(slots, weights):
    columns = jnp.arange(E_WIN * CAP, dtype=jnp.int32)
    match = (slots[:, :, None] == columns[None, None, :]).astype(jnp.float32)
    return jnp.sum(weights[:, :, None] * match, axis=1)


def pick_rows(table, token_rows):
    return jnp.einsum(
        "tc,td->cd", table.astype(jnp.bfloat16), token_rows, preferred_element_type=jnp.float32
    ).astype(jnp.bfloat16)


def fan_out(buffer, group_size):
    return jnp.repeat(buffer.reshape(E_WIN, CAP, buffer.shape[-1]), group_size, axis=0)


def partial_total(returned_parts, group_size):
    width = returned_parts.shape[-1]
    summed = returned_parts.reshape(E_WIN, group_size, CAP, width).astype(jnp.float32).sum(axis=1)
    return summed.reshape(E_WIN * CAP, width)


def token_sum(totals, slots, weights):
    picked = jnp.take(totals, slots.reshape(-1), axis=0).reshape(
        slots.shape[0], slots.shape[1], totals.shape[-1]
    )
    return jnp.sum(weights[:, :, None] * picked, axis=1)


def body(
    carried, saved_rows, returned, fwd_ids, fwd_gates, bwd_ids, bwd_gates, gate_w, up_w, down_w
):
    devices = lax.axis_size("expert")
    group_size = devices // E_WIN
    layer_in = passed_along(carried, "section", 1)[0]
    cotangent = passed_along(returned, "section", -1)[0]
    saved_in = saved_rows[0]
    fwd_route = fwd_ids[0]
    bwd_route = bwd_ids[0]
    fwd_weight = fwd_gates[0]
    bwd_weight = bwd_gates[0]
    gate_part = gate_w[0]
    up_part = up_w[0]
    down_part = down_w[0]
    width = layer_in.shape[1]
    fwd_slots = slot_table(fwd_route)
    bwd_slots = slot_table(bwd_route)
    fwd_ones = spread(fwd_slots, jnp.ones(fwd_weight.shape, jnp.float32))
    bwd_ones = spread(bwd_slots, jnp.ones(bwd_weight.shape, jnp.float32))
    slot_gates = jnp.sum(spread(bwd_slots, bwd_weight), axis=0)
    send_rows = fan_out(pick_rows(fwd_ones, layer_in), group_size)
    recv_rows = lax.all_to_all(send_rows, "expert", split_axis=0, concat_axis=0, tiled=True)
    send_saved = fan_out(pick_rows(bwd_ones, saved_in), group_size)
    chosen_grads = pick_rows(bwd_ones, cotangent)
    gated = (slot_gates[:, None] * chosen_grads.astype(jnp.float32)).astype(jnp.bfloat16)
    send_scaled = fan_out(gated, group_size)
    recv_saved, recv_scaled = (
        lax.all_to_all(send_saved, "expert", split_axis=0, concat_axis=0, tiled=True),
        lax.all_to_all(send_scaled, "expert", split_axis=0, concat_axis=0, tiled=True),
    )
    token_rows = recv_rows.reshape(-1, width)
    pre_gate = jnp.dot(token_rows, gate_part, preferred_element_type=jnp.float32)
    pre_up = jnp.dot(token_rows, up_part, preferred_element_type=jnp.float32)
    hidden = (pre_gate * jax.nn.sigmoid(pre_gate) * pre_up).astype(jnp.bfloat16)
    fwd_parts = (
        jnp.dot(hidden, down_part, preferred_element_type=jnp.float32)
        .astype(jnp.bfloat16)
        .reshape(devices, CAP, width)
    )
    saved_flat = recv_saved.reshape(-1, width)
    scaled_flat = recv_scaled.reshape(-1, width)
    pre_gate2 = jnp.dot(saved_flat, gate_part, preferred_element_type=jnp.float32)
    pre_up2 = jnp.dot(saved_flat, up_part, preferred_element_type=jnp.float32)
    sigma2 = jax.nn.sigmoid(pre_gate2)
    swish = pre_gate2 * sigma2
    hidden2 = (swish * pre_up2).astype(jnp.bfloat16)
    grad_hidden = jnp.einsum(
        "rd,hd->rh", scaled_flat, down_part, preferred_element_type=jnp.float32
    )
    grad_gate_pre = (grad_hidden * pre_up2 * sigma2 * (1.0 + pre_gate2 * (1.0 - sigma2))).astype(
        jnp.bfloat16
    )
    grad_up_pre = (grad_hidden * swish).astype(jnp.bfloat16)
    back_parts = jnp.einsum(
        "rh,dh->rd", grad_gate_pre, gate_part, preferred_element_type=jnp.float32
    )
    back_parts = back_parts + jnp.einsum(
        "rh,dh->rd", grad_up_pre, up_part, preferred_element_type=jnp.float32
    )
    back_parts = back_parts.astype(jnp.bfloat16).reshape(devices, CAP, width)
    gate_grad = jnp.einsum(
        "rd,rh->dh", saved_flat, grad_gate_pre, preferred_element_type=jnp.float32
    )
    up_grad = jnp.einsum("rd,rh->dh", saved_flat, grad_up_pre, preferred_element_type=jnp.float32)
    down_grad = jnp.einsum("rh,rd->hd", hidden2, scaled_flat, preferred_element_type=jnp.float32)
    fwd_back = lax.all_to_all(fwd_parts, "expert", split_axis=0, concat_axis=0, tiled=True)
    bwd_back = lax.all_to_all(back_parts, "expert", split_axis=0, concat_axis=0, tiled=True)
    output_sum = layer_in.astype(jnp.float32) + token_sum(
        partial_total(fwd_back, group_size), fwd_slots, fwd_weight
    )
    input_grad = cotangent.astype(jnp.float32) + token_sum(
        partial_total(bwd_back, group_size), bwd_slots, jnp.ones(bwd_weight.shape, jnp.float32)
    )
    return (
        output_sum.astype(jnp.bfloat16)[None],
        input_grad.astype(jnp.bfloat16)[None],
        gate_grad[None],
        up_grad[None],
        down_grad[None],
    )


def solution(mesh):
    placed = (
        P("section", "expert", None),
        P("section", "expert", None),
        P("section", "expert", None),
        P("section", "expert", None),
        P("section", "expert", None),
        P("section", "expert", None),
        P("section", "expert", None),
        P("section", None, "expert"),
        P("section", None, "expert"),
        P("section", "expert", None),
    )
    return jax.shard_map(
        body,
        mesh=mesh,
        in_specs=placed,
        out_specs=(
            P("section", "expert", None),
            P("section", "expert", None),
            P("section", None, "expert"),
            P("section", None, "expert"),
            P("section", "expert", None),
        ),
        check_vma=False,
    )
```

```python
import jax
import jax.numpy as jnp
from jax import lax
from jax.experimental import pallas as pl
from jax.experimental.pallas import tpu as pltpu
from jax.sharding import PartitionSpec as P

E_WIN = 4
TOK = 128
CHIP = 2 * TOK
SLOT = 144
D = 2048
HALF = D // 2
QUART = D // 4
HID = 256
SAVED, FWD, COT = 0, 1, 2
N_COPY = 160
MESH = pl.DeviceIdType.MESH
F32 = jnp.float32
BF16 = jnp.bfloat16


def contract(a, b, dims):
    return lax.dot_general(a, b, ((dims[:1], dims[1:]), ((), ())), preferred_element_type=F32)


def kernel(
    carried, saved, returned, routes, gate_h, up_h, down_h,
    nxt, gin, gate_o, up_o, down_o,
    tok, toky, pack_a, pack_b, rows, gate, up, down, rts, pick, gates,
    keep_f, part_f, sum_in, ret_y, ret_a, ret_b, mix_out, mix_in, fin,
    swish_s, slope_s, hid2_s, pre_s, grad_s, grad_d, ss, rs, ls,
):
    s, r = lax.axis_index("section"), lax.axis_index("expert")
    x, yh, c = r // 4, (r // 2) % 2, r % 2
    oy, oc = 1 - yh, 1 - c
    core_dev = (s, x * 4 + yh * 2 + oc)
    y_dev = (s, x * 4 + oy * 2 + c)
    diag_dev = (s, x * 4 + oy * 2 + oc)

    def x_at(j):
        return lax.rem(x + j, 4)

    def x_dev(j):
        return (s, x_at(j) * 4 + yh * 2 + c)

    def sec_dev(step, dc):
        return (lax.rem(s + step + 16, 16), x * 4 + yh * 2 + lax.rem(c + dc, 2))

    count = [0]
    locals_ = [0]
    pending = []

    def send(src, dst, dev):
        i = count[0]
        count[0] += 1
        copy = pltpu.make_async_remote_copy(
            src_ref=src, dst_ref=dst, send_sem=ss.at[i], recv_sem=rs.at[i], device_id=dev, device_id_type=MESH
        )
        copy.start()
        pending.append(copy)
        return i, copy

    def arrive(i, land, dev):
        pltpu.make_async_remote_copy(
            src_ref=land, dst_ref=land, send_sem=ss.at[i], recv_sem=rs.at[i], device_id=dev, device_id_type=MESH
        ).wait_recv()

    def sent(copy):
        copy.wait_send()
        pending[:] = [other for other in pending if other is not copy]

    def local(src, dst):
        copy = pltpu.make_async_copy(src, dst, ls.at[locals_[0]])
        locals_[0] += 1
        copy.start()
        return copy

    def cols(core, quarter):
        return pl.ds(pl.multiple_of(core * HALF + quarter * QUART, QUART), QUART)

    def half(core):
        return pl.ds(pl.multiple_of(core * HALF, HALF), HALF)

    def lines(core):
        return pl.ds(pl.multiple_of(core * TOK, TOK), TOK)

    barrier = pltpu.get_barrier_semaphore()
    greeted = [core_dev, y_dev, diag_dev, x_dev(1), x_dev(2), x_dev(3), sec_dev(1, 0), sec_dev(1, 1), sec_dev(-1, 0), sec_dev(-1, 1)]
    own_half = local(saved.at[:, half(c)], tok.at[SAVED, lines(c), :])
    weights = [local(gate_h, gate), local(up_h, up), local(down_h, down)]
    for dev in greeted:
        pl.semaphore_signal(barrier, inc=1, device_id=dev, device_id_type=MESH)
    pl.semaphore_wait(barrier, len(greeted))
    i_saved, _ = send(saved.at[:, half(oc)], tok.at[SAVED, lines(c), :], core_dev)
    i_r1, _ = send(routes, rts.at[c], core_dev)
    i_r2, _ = send(routes, rts.at[2 + c], y_dev)
    i_r3, _ = send(routes, rts.at[2 + c], diag_dev)
    i_carry = [send(carried.at[:, half(lax.rem(c + dc, 2))], tok.at[FWD, lines(c), :], sec_dev(1, dc))[0] for dc in (0, 1)]
    i_back = [send(returned.at[:, half(lax.rem(c + dc, 2))], tok.at[COT, lines(c), :], sec_dev(-1, dc))[0] for dc in (0, 1)]
    rts[pl.ds(c, 1)] = routes[...][None]
    arrive(i_r1, rts.at[oc], core_dev)
    arrive(i_r2, rts.at[2 + c], y_dev)
    arrive(i_r3, rts.at[2 + oc], diag_dev)

    expert_of = lax.broadcasted_iota(jnp.int32, (8, CHIP), 0).astype(F32)
    slot_of = lax.broadcasted_iota(jnp.int32, (SLOT, CHIP), 0).astype(F32)
    earlier = (
        lax.broadcasted_iota(jnp.int32, (CHIP, CHIP), 0) < lax.broadcasted_iota(jnp.int32, (CHIP, CHIP), 1)
    ).astype(F32).astype(BF16)

    def table(where, way):
        listed = jnp.concatenate([rts[2 * where], rts[2 * where + 1]], axis=1)
        b = 4 * way
        first, second = listed[b : b + 1] == expert_of, listed[b + 1 : b + 2] == expert_of
        chosen = jnp.logical_or(first, second)
        gates[where, way] = jnp.where(first, listed[b + 2 : b + 3], jnp.where(second, listed[b + 3 : b + 4], 0.0))
        rank = jnp.dot(chosen.astype(F32).astype(BF16), earlier, preferred_element_type=F32)
        rank = jnp.where(chosen, rank, -1.0)
        for e in range(E_WIN):
            pick[where, way, e] = (slot_of == rank[e : e + 1]).astype(F32).astype(BF16)

    def picked(what, where, e, tokens):
        way = 0 if what == FWD else 1
        table_e = pick[where, way, e]
        block = jnp.dot(table_e, tokens, preferred_element_type=F32)
        if what == COT:
            gate_e = gates[where, way, pl.ds(e, 1), :]
            block = block * jnp.sum(table_e.astype(F32) * gate_e, axis=1, keepdims=True)
        return block.astype(BF16)

    ids = {}

    def stage1(t):
        ids[t, "b1"] = send(tok.at[t, :, pl.ds(QUART, QUART)], toky.at[t], y_dev)[0]
        for j in (2, 1, 3, 0):
            block = picked(t, 0, x_at(j), tok[t, :, :QUART])
            if j:
                pack_a[t, j - 1] = block
                ids[t, "xa", j] = send(pack_a.at[t, j - 1], rows.at[t, yh, x, :, cols(c, 0)], x_dev(j))[0]
            else:
                rows[t, yh, x, :, cols(c, 0)] = block

    def stage2(t):
        arrive(ids[t, "b1"], toky.at[t], y_dev)
        for j in (2, 1, 3, 0):
            for where, hh in ((0, yh), (1, oy)):
                tokens = tok[t, :, QUART:] if where == 0 else toky[t]
                block = picked(t, where, x_at(j), tokens)
                if j:
                    pack_b[t, j - 1, hh] = block
                else:
                    rows[t, hh, x, :, cols(c, 1)] = block
            if j:
                ids[t, "xb", j] = send(pack_b.at[t, j - 1], rows.at[t, :, x, :, cols(c, 1)], x_dev(j))[0]
        for j in (0, 1, 3, 2):
            place = rows.at[t, yh, x_at(4 - j), :, cols(c, 0)]
            if j:
                arrive(ids[t, "xa", j], place, x_dev(4 - j))
            ids[t, "ya", j] = send(place, place, y_dev)
        place = rows.at[t, yh, :, :, cols(c, 0)]
        ids[t, "c0"] = send(place, place, core_dev)

    def stage3(t):
        for j in (0, 1, 3, 2):
            arrive(ids[t, "ya", j][0], rows.at[t, oy, x_at(4 - j), :, cols(c, 0)], y_dev)
        place = rows.at[t, oy, :, :, cols(c, 0)]
        ids[t, "c1"] = send(place, place, core_dev)
        for j in (1, 3, 2):
            arrive(ids[t, "xb", j], rows.at[t, :, x_at(4 - j), :, cols(c, 1)], x_dev(4 - j))
        place = rows.at[t, :, :, :, cols(c, 1)]
        ids[t, "c2"] = send(place, place, core_dev)

    def stage4(t):
        arrive(ids[t, "c0"][0], rows.at[t, yh, :, :, cols(oc, 0)], core_dev)
        arrive(ids[t, "c1"][0], rows.at[t, oy, :, :, cols(oc, 0)], core_dev)
        arrive(ids[t, "c2"][0], rows.at[t, :, :, :, cols(oc, 1)], core_dev)

    def group(t, hh):
        return rows[t, hh].reshape(E_WIN * SLOT, D)

    keep = (keep_f, rows.at[FWD, :, :, :, pl.ds(0, HALF)])
    part = (part_f, rows.at[FWD, :, :, :, pl.ds(HALF, HALF)])

    def share(way, hh):
        ids[way, "cs", hh is yh] = send(part[way].at[hh], sum_in.at[way, hh], core_dev)[0]

    def forward(hh):
        token_rows = group(FWD, hh)
        pre_gate = jnp.dot(token_rows, gate[...], preferred_element_type=F32)
        pre_up = jnp.dot(token_rows, up[...], preferred_element_type=F32)
        hidden = (pre_gate * jax.nn.sigmoid(pre_gate) * pre_up).astype(BF16)
        for buffer, core in ((part_f, oc), (keep_f, c)):
            out = jnp.dot(hidden, down[:, half(core)], preferred_element_type=F32)
            buffer[hh] = out.astype(BF16).reshape(E_WIN, SLOT, HALF)
            if core is oc:
                share(0, hh)

    def before(hh):
        token_rows = group(SAVED, hh)
        pre_gate = jnp.dot(token_rows, gate[...], preferred_element_type=F32)
        pre_up = jnp.dot(token_rows, up[...], preferred_element_type=F32)
        sig = jax.nn.sigmoid(pre_gate)
        swish = pre_gate * sig
        swish_s[hh] = swish
        slope_s[hh] = pre_up * sig * (1.0 + pre_gate * (1.0 - sig))
        hid2_s[hh] = (swish * pre_up).astype(BF16)

    def backward(hh):
        grad_hidden = contract(group(COT, hh), down[...], (1, 1))
        grad_gate = (grad_hidden * slope_s[hh]).astype(BF16)
        grad_up = (grad_hidden * swish_s[hh]).astype(BF16)
        pre_s[hh, :, :HID] = grad_gate
        pre_s[hh, :, HID:] = grad_up
        for buffer, core in ((part[1], oc), (keep[1], c)):
            out = contract(grad_gate, gate[half(core), :], (1, 1)) + contract(grad_up, up[half(core), :], (1, 1))
            buffer[hh] = out.astype(BF16).reshape(E_WIN, SLOT, HALF)
            if core is oc:
                share(1, hh)

    def add_core(way, hh):
        arrive(ids[way, "cs", hh is yh], sum_in.at[way, hh], core_dev)
        keep[way][hh] = (keep[way][hh].astype(F32) + sum_in[way, hh].astype(F32)).astype(BF16)

    def return1(way):
        add_core(way, oy)
        ids[way, "ry"] = send(keep[way].at[oy, :, :, pl.ds(0, QUART)], ret_y.at[way], y_dev)[0]
        add_core(way, yh)
        for j in (2, 1, 3):
            ids[way, "rb", j] = send(keep[way].at[:, x_at(j), :, pl.ds(QUART, QUART)], ret_b.at[way, :, x], x_dev(j))[0]
        ret_b[way, :, x] = keep[way][:, x, :, QUART:]

    def return2(way):
        arrive(ids[way, "ry"], ret_y.at[way], y_dev)
        both = keep[way][yh, :, :, :QUART].astype(F32) + ret_y[way].astype(F32)
        keep[way][yh, :, :, :QUART] = both.astype(BF16)
        for j in (2, 1, 3):
            ids[way, "ra", j] = send(keep[way].at[yh, x_at(j), :, pl.ds(0, QUART)], ret_a.at[way, x], x_dev(j))[0]
        ret_a[way, x] = keep[way][yh, x, :, :QUART]

    def mixed(way, where, block):
        block = block.reshape(E_WIN * SLOT, QUART)
        table_all = pick[where, way].astype(F32)
        if way == 1:
            return contract(table_all.reshape(E_WIN * SLOT, CHIP).astype(BF16), block, (0, 0))
        weight = gates[where, way][:E_WIN]
        coarse = weight.astype(BF16).astype(F32)
        fine = weight - coarse
        coarse = (table_all * coarse[:, None, :]).reshape(E_WIN * SLOT, CHIP).astype(BF16)
        fine = (table_all * fine[:, None, :]).reshape(E_WIN * SLOT, CHIP).astype(BF16)
        return contract(coarse, block, (0, 0)) + contract(fine, block, (0, 0))

    def return3(way):
        t = FWD if way == 0 else COT
        for j in (1, 3, 2):
            arrive(ids[way, "rb", j], ret_b.at[way, :, x_at(4 - j)], x_dev(4 - j))
        mix_out[way] = mixed(way, 1, ret_b[way, oy]).astype(BF16)
        i = send(mix_out.at[way], mix_in.at[way], y_dev)[0]
        total = tok[t, :, QUART:].astype(F32) + mixed(way, 0, ret_b[way, yh])
        for j in (1, 3, 2):
            arrive(ids[way, "ra", j], ret_a.at[way, x_at(4 - j)], x_dev(4 - j))
        fin[way, :, :QUART] = (tok[t, :, :QUART].astype(F32) + mixed(way, 0, ret_a[way])).astype(BF16)
        arrive(i, mix_in.at[way], y_dev)
        fin[way, :, QUART:] = (total + mix_in[way].astype(F32)).astype(BF16)
        out = (nxt, gin)[way]
        ids[way, "out"] = send(fin.at[way, lines(oc), :], out.at[:, half(c)], core_dev)[0]
        ids[way, "mine"] = local(fin.at[way, lines(c), :], out.at[:, half(c)])

    def weight_grads():
        step = 512

        def one(k, carry):
            place = pl.ds(pl.multiple_of(k * step, step), step)
            lhs = rows[SAVED, :, :, :, place].reshape(2 * E_WIN * SLOT, step)
            grad_s[place, :] = contract(lhs, pre_s[...].reshape(2 * E_WIN * SLOT, 2 * HID), (0, 0))
            rhs = rows[COT, :, :, :, place].reshape(2 * E_WIN * SLOT, step)
            grad_d[:, place] = contract(hid2_s[...].reshape(2 * E_WIN * SLOT, HID), rhs, (0, 0))
            return carry

        lax.fori_loop(0, D // step, one, 0)
        return [local(grad_s.at[:, pl.ds(0, HID)], gate_o), local(grad_s.at[:, pl.ds(HID, HID)], up_o), local(grad_d, down_o)]

    table(0, 1)
    own_half.wait()
    arrive(i_saved, tok.at[SAVED, lines(oc), :], core_dev)
    stage1(SAVED)
    table(1, 1)
    table(0, 0)
    table(1, 0)
    stage2(SAVED)
    for dc in (0, 1):
        arrive(i_carry[dc], tok.at[FWD, lines(lax.rem(c + dc, 2)), :], sec_dev(-1, dc))
    stage1(FWD)
    stage3(SAVED)
    stage2(FWD)
    for copy in weights:
        copy.wait()
    stage4(SAVED)
    before(oy)
    before(yh)
    for dc in (0, 1):
        arrive(i_back[dc], tok.at[COT, lines(lax.rem(c + dc, 2)), :], sec_dev(1, dc))
    stage1(COT)
    stage3(FWD)
    stage2(COT)
    stage4(FWD)
    forward(oy)
    forward(yh)
    return1(0)
    return2(0)
    stage3(COT)
    stage4(COT)
    for key in [("c0"), ("c1"), ("c2")]:
        sent(ids[FWD, key][1])
    for j in range(4):
        sent(ids[FWD, "ya", j][1])
    backward(oy)
    backward(yh)
    return1(1)
    return2(1)
    return3(0)
    grads_out = weight_grads()
    return3(1)
    for way, out in ((0, nxt), (1, gin)):
        arrive(ids[way, "out"], out.at[:, half(oc)], core_dev)
        ids[way, "mine"].wait()
    for copy in grads_out:
        copy.wait()
    for copy in list(pending):
        copy.wait_send()


def body(carried, saved_rows, returned, fwd_ids, fwd_gates, bwd_ids, bwd_gates, gate_w, up_w, down_w):
    routes = jnp.concatenate([fwd_ids[0].astype(F32), fwd_gates[0], bwd_ids[0].astype(F32), bwd_gates[0]], axis=1).T
    whole = pl.BlockSpec(memory_space=pl.ANY)
    group_rows = E_WIN * SLOT
    scratch = [
        pltpu.VMEM((3, CHIP, HALF), BF16),
        pltpu.VMEM((3, CHIP, QUART), BF16),
        pltpu.VMEM((3, 3, SLOT, QUART), BF16),
        pltpu.VMEM((3, 3, 2, SLOT, QUART), BF16),
        pltpu.VMEM((3, 2, E_WIN, SLOT, D), BF16),
        pltpu.VMEM((D, HID), BF16),
        pltpu.VMEM((D, HID), BF16),
        pltpu.VMEM((HID, D), BF16),
        pltpu.VMEM((4, 8, TOK), F32),
        pltpu.VMEM((2, 2, E_WIN, SLOT, CHIP), BF16),
        pltpu.VMEM((2, 2, 8, CHIP), F32),
        pltpu.VMEM((2, E_WIN, SLOT, HALF), BF16),
        pltpu.VMEM((2, E_WIN, SLOT, HALF), BF16),
        pltpu.VMEM((2, 2, E_WIN, SLOT, HALF), BF16),
        pltpu.VMEM((2, E_WIN, SLOT, QUART), BF16),
        pltpu.VMEM((2, E_WIN, SLOT, QUART), BF16),
        pltpu.VMEM((2, 2, E_WIN, SLOT, QUART), BF16),
        pltpu.VMEM((2, CHIP, QUART), BF16),
        pltpu.VMEM((2, CHIP, QUART), BF16),
        pltpu.VMEM((2, CHIP, HALF), BF16),
        pltpu.VMEM((2, group_rows, HID), F32),
        pltpu.VMEM((2, group_rows, HID), F32),
        pltpu.VMEM((2, group_rows, HID), BF16),
        pltpu.VMEM((2, group_rows, 2 * HID), BF16),
        pltpu.VMEM((D, 2 * HID), F32),
        pltpu.VMEM((HID, D), F32),
        pltpu.SemaphoreType.DMA((N_COPY,)),
        pltpu.SemaphoreType.DMA((N_COPY,)),
        pltpu.SemaphoreType.DMA((16,)),
    ]
    rows_all = 2 * group_rows
    outs = pl.pallas_call(
        kernel,
        name="relay_tick",
        out_shape=(
            jax.ShapeDtypeStruct((TOK, D), BF16),
            jax.ShapeDtypeStruct((TOK, D), BF16),
            jax.ShapeDtypeStruct((D, HID), F32),
            jax.ShapeDtypeStruct((D, HID), F32),
            jax.ShapeDtypeStruct((HID, D), F32),
        ),
        in_specs=[whole] * 3 + [pl.BlockSpec(memory_space=pltpu.VMEM)] + [whole] * 3,
        out_specs=(whole,) * 5,
        scratch_shapes=scratch,
        compiler_params=pltpu.CompilerParams(collective_id=0, has_side_effects=True, vmem_limit_bytes=60 * 2**20),
        cost_estimate=pl.CostEstimate(flops=2 * rows_all * D * 2816, bytes_accessed=12 * 2**20, transcendentals=2 * rows_all * HID),
    )(carried[0], saved_rows[0], returned[0], routes, gate_w[0], up_w[0], down_w[0])
    return tuple(out[None] for out in outs)


def solution(mesh):
    tokens = P("section", "expert", None)
    columns = P("section", None, "expert")
    return jax.shard_map(
        body,
        mesh=mesh,
        in_specs=(tokens,) * 7 + (columns, columns, tokens),
        out_specs=(tokens, tokens, columns, columns, tokens),
        check_vma=False,
    )
```

```python
import jax
import jax.numpy as jnp
from jax import lax
from jax.experimental import pallas as pl
from jax.experimental.pallas import tpu as pltpu
from jax.sharding import PartitionSpec as P

E_WIN = 4
TOK = 128
CHIP = 2 * TOK
SLOT = 144
D = 2048
HALF = D // 2
QUART = D // 4
HID = 256
SAVED, FWD, COT = 0, 1, 2
N_COPY = 160
MESH = pl.DeviceIdType.MESH
F32 = jnp.float32
BF16 = jnp.bfloat16


def contract(a, b, dims):
    return lax.dot_general(a, b, ((dims[:1], dims[1:]), ((), ())), preferred_element_type=F32)


def kernel(
    carried, saved, returned, fwd_ids, fwd_gates, bwd_ids, bwd_gates, gate_h, up_h, down_h,
    nxt, gin, gate_o, up_o, down_o,
    tok, toky, pack_a, pack_b, rows, gate, up, down, routes, rts, pick, gates,
    keep_b, part_b, sum_in, ret_y, ret_a, ret_b, mix_out, mix_in, fin,
    swish_s, slope_s, hid2_s, pre_s, ss, rs, ls,
):
    s, r = lax.axis_index("section"), lax.axis_index("expert")
    x, yh, c = r // 4, (r // 2) % 2, r % 2
    oy, oc = 1 - yh, 1 - c
    core_dev = (s, x * 4 + yh * 2 + oc)
    y_dev = (s, x * 4 + oy * 2 + c)
    diag_dev = (s, x * 4 + oy * 2 + oc)

    def x_at(j):
        return lax.rem(x + j, 4)

    def x_dev(j):
        return (s, x_at(j) * 4 + yh * 2 + c)

    def sec_dev(step, dc):
        return (lax.rem(s + step + 16, 16), x * 4 + yh * 2 + lax.rem(c + dc, 2))

    count = [0]
    locals_ = [0]
    pending = []

    def send(src, dst, dev):
        i = count[0]
        count[0] += 1
        copy = pltpu.make_async_remote_copy(
            src_ref=src, dst_ref=dst, send_sem=ss.at[i], recv_sem=rs.at[i], device_id=dev, device_id_type=MESH
        )
        copy.start()
        pending.append(copy)
        return i, copy

    def arrive(i, land, dev):
        pltpu.make_async_remote_copy(
            src_ref=land, dst_ref=land, send_sem=ss.at[i], recv_sem=rs.at[i], device_id=dev, device_id_type=MESH
        ).wait_recv()

    def sent(copy):
        copy.wait_send()
        pending[:] = [other for other in pending if other is not copy]

    def local(src, dst):
        copy = pltpu.make_async_copy(src, dst, ls.at[locals_[0]])
        locals_[0] += 1
        copy.start()
        return copy

    def cols(core, quarter):
        return pl.ds(pl.multiple_of(core * HALF + quarter * QUART, QUART), QUART)

    def half(core):
        return pl.ds(pl.multiple_of(core * HALF, HALF), HALF)

    def lines(core):
        return pl.ds(pl.multiple_of(core * TOK, TOK), TOK)

    barrier = pltpu.get_barrier_semaphore()
    greeted = [core_dev, y_dev, diag_dev, x_dev(1), x_dev(2), x_dev(3), sec_dev(1, 0), sec_dev(1, 1), sec_dev(-1, 0), sec_dev(-1, 1)]
    own_half = local(saved.at[:, half(c)], tok.at[SAVED, lines(c), :])
    weights = [local(gate_h, gate), local(up_h, up), local(down_h, down)]
    for row, numbers in enumerate((fwd_ids, fwd_gates, bwd_ids, bwd_gates)):
        routes[2 * row : 2 * row + 2, :] = numbers[...].astype(F32)
    for dev in greeted:
        pl.semaphore_signal(barrier, inc=1, device_id=dev, device_id_type=MESH)
    pl.semaphore_wait(barrier, len(greeted))
    i_r1, _ = send(routes, rts.at[c], core_dev)
    i_r2, _ = send(routes, rts.at[2 + c], y_dev)
    i_r3, _ = send(routes, rts.at[2 + c], diag_dev)
    i_saved, _ = send(saved.at[:, half(oc)], tok.at[SAVED, lines(c), :], core_dev)
    i_b1 = [
        send(saved.at[:, cols(c, 1)], toky.at[SAVED, lines(c), :], y_dev)[0],
        send(saved.at[:, cols(oc, 1)], toky.at[SAVED, lines(c), :], diag_dev)[0],
    ]
    i_back = [send(returned.at[:, half(lax.rem(c + dc, 2))], tok.at[COT, lines(c), :], sec_dev(-1, dc))[0] for dc in (0, 1)]
    i_carry = [send(carried.at[:, half(lax.rem(c + dc, 2))], tok.at[FWD, lines(c), :], sec_dev(1, dc))[0] for dc in (0, 1)]
    rts[pl.ds(c, 1)] = routes[...][None]

    expert_of = lax.broadcasted_iota(jnp.int32, (8, CHIP), 0).astype(F32)
    slot_of = lax.broadcasted_iota(jnp.int32, (SLOT, CHIP), 0).astype(F32)
    earlier = (
        lax.broadcasted_iota(jnp.int32, (CHIP, CHIP), 0) < lax.broadcasted_iota(jnp.int32, (CHIP, CHIP), 1)
    ).astype(F32).astype(BF16)

    def table(where, way):
        listed = jnp.concatenate([rts[2 * where], rts[2 * where + 1]], axis=1)
        b = 4 * way
        first, second = listed[b : b + 1] == expert_of, listed[b + 1 : b + 2] == expert_of
        chosen = jnp.logical_or(first, second)
        gates[where, way] = jnp.where(first, listed[b + 2 : b + 3], jnp.where(second, listed[b + 3 : b + 4], 0.0))
        rank = jnp.dot(chosen.astype(F32).astype(BF16), earlier, preferred_element_type=F32)
        rank = jnp.where(chosen, rank, -1.0)
        for e in range(E_WIN):
            pick[where, way, e] = (slot_of == rank[e : e + 1]).astype(F32).astype(BF16)

    def picked(what, where, e, tokens):
        way = 0 if what == FWD else 1
        table_e = pick[where, way, e]
        block = jnp.dot(table_e, tokens, preferred_element_type=F32)
        if what == COT:
            gate_e = gates[where, way, pl.ds(e, 1), :]
            block = block * jnp.sum(table_e.astype(F32) * gate_e, axis=1, keepdims=True)
        return block.astype(BF16)

    ids = {}

    def stage1(t):
        if t != SAVED:
            ids[t, "b1"] = send(tok.at[t, :, pl.ds(QUART, QUART)], toky.at[t], y_dev)[0]
        for j in (2, 1, 3, 0):
            block = picked(t, 0, x_at(j), tok[t, :, :QUART])
            if j:
                pack_a[t, j - 1] = block
                ids[t, "xa", j] = send(pack_a.at[t, j - 1], rows.at[t, yh, x, :, cols(c, 0)], x_dev(j))[0]
            else:
                rows[t, yh, x, :, cols(c, 0)] = block

    def stage2(t):
        if t == SAVED:
            arrive(i_b1[0], toky.at[t, lines(c), :], y_dev)
            arrive(i_b1[1], toky.at[t, lines(oc), :], diag_dev)
        else:
            arrive(ids[t, "b1"], toky.at[t], y_dev)
        for j in (2, 1, 3, 0):
            for where, hh in ((0, yh), (1, oy)):
                tokens = tok[t, :, QUART:] if where == 0 else toky[t]
                block = picked(t, where, x_at(j), tokens)
                if j:
                    pack_b[t, j - 1, hh] = block
                else:
                    rows[t, hh, x, :, cols(c, 1)] = block
            if j:
                ids[t, "xb", j] = send(pack_b.at[t, j - 1], rows.at[t, :, x, :, cols(c, 1)], x_dev(j))[0]
        for j in (0, 1, 3, 2):
            place = rows.at[t, yh, x_at(4 - j), :, cols(c, 0)]
            if j:
                arrive(ids[t, "xa", j], place, x_dev(4 - j))
            ids[t, "ya", j] = send(place, place, y_dev)
        place = rows.at[t, yh, :, :, cols(c, 0)]
        ids[t, "c0"] = send(place, place, core_dev)

    def stage3(t):
        for j in (0, 1, 3, 2):
            arrive(ids[t, "ya", j][0], rows.at[t, oy, x_at(4 - j), :, cols(c, 0)], y_dev)
        place = rows.at[t, oy, :, :, cols(c, 0)]
        ids[t, "c1"] = send(place, place, core_dev)
        for j in (1, 3, 2):
            arrive(ids[t, "xb", j], rows.at[t, :, x_at(4 - j), :, cols(c, 1)], x_dev(4 - j))
        place = rows.at[t, :, :, :, cols(c, 1)]
        ids[t, "c2"] = send(place, place, core_dev)

    def stage4(t):
        arrive(ids[t, "c0"][0], rows.at[t, yh, :, :, cols(oc, 0)], core_dev)
        arrive(ids[t, "c1"][0], rows.at[t, oy, :, :, cols(oc, 0)], core_dev)
        arrive(ids[t, "c2"][0], rows.at[t, :, :, :, cols(oc, 1)], core_dev)

    def group(t, hh):
        return rows[t, hh].reshape(E_WIN * SLOT, D)

    keep = (rows.at[FWD, :, :, :, pl.ds(0, HALF)], keep_b)
    part = (rows.at[FWD, :, :, :, pl.ds(HALF, HALF)], part_b)

    def share(way, hh):
        ids[way, "cs", hh is yh] = send(part[way].at[hh], sum_in.at[way, hh], core_dev)[0]

    def forward(hh):
        token_rows = group(FWD, hh)
        pre_gate = jnp.dot(token_rows, gate[...], preferred_element_type=F32)
        pre_up = jnp.dot(token_rows, up[...], preferred_element_type=F32)
        hidden = (pre_gate * jax.nn.sigmoid(pre_gate) * pre_up).astype(BF16)
        for buffer, core in ((part[0], oc), (keep[0], c)):
            out = jnp.dot(hidden, down[:, half(core)], preferred_element_type=F32)
            buffer[hh] = out.astype(BF16).reshape(E_WIN, SLOT, HALF)
            if core is oc:
                share(0, hh)

    def before(hh):
        token_rows = group(SAVED, hh)
        pre_gate = jnp.dot(token_rows, gate[...], preferred_element_type=F32)
        pre_up = jnp.dot(token_rows, up[...], preferred_element_type=F32)
        sig = jax.nn.sigmoid(pre_gate)
        swish = pre_gate * sig
        swish_s[hh] = swish
        slope_s[hh] = pre_up * sig * (1.0 + pre_gate * (1.0 - sig))
        hid2_s[hh] = (swish * pre_up).astype(BF16)

    def backward(hh):
        grad_hidden = contract(group(COT, hh), down[...], (1, 1))
        grad_gate = (grad_hidden * slope_s[hh]).astype(BF16)
        grad_up = (grad_hidden * swish_s[hh]).astype(BF16)
        pre_s[hh, :, :HID] = grad_gate
        pre_s[hh, :, HID:] = grad_up
        for buffer, core in ((part[1], oc), (keep[1], c)):
            out = contract(grad_gate, gate[half(core), :], (1, 1)) + contract(grad_up, up[half(core), :], (1, 1))
            buffer[hh] = out.astype(BF16).reshape(E_WIN, SLOT, HALF)
            if core is oc:
                share(1, hh)

    def add_core(way, hh):
        arrive(ids[way, "cs", hh is yh], sum_in.at[way, hh], core_dev)
        keep[way][hh] = (keep[way][hh].astype(F32) + sum_in[way, hh].astype(F32)).astype(BF16)

    def return1(way):
        for where, hh in ((1, oy), (0, yh)):
            add_core(way, hh)
            if where:
                ids[way, "ry"] = send(keep[way].at[oy, :, :, pl.ds(0, QUART)], ret_y.at[way], y_dev)[0]
            for j in (2, 1, 3):
                ids[way, "rb", where, j] = send(
                    keep[way].at[hh, x_at(j), :, pl.ds(QUART, QUART)], ret_b.at[way, hh, x], x_dev(j)
                )[0]
            ret_b[way, hh, x] = keep[way][hh, x, :, QUART:]

    def return2(way):
        arrive(ids[way, "ry"], ret_y.at[way], y_dev)
        both = keep[way][yh, :, :, :QUART].astype(F32) + ret_y[way].astype(F32)
        keep[way][yh, :, :, :QUART] = both.astype(BF16)
        for j in (2, 1, 3):
            ids[way, "ra", j] = send(keep[way].at[yh, x_at(j), :, pl.ds(0, QUART)], ret_a.at[way, x], x_dev(j))[0]
        ret_a[way, x] = keep[way][yh, x, :, :QUART]

    def mixed(way, where, block):
        block = block.reshape(E_WIN * SLOT, QUART)
        table_all = pick[where, way].astype(F32)
        if way == 1:
            return contract(table_all.reshape(E_WIN * SLOT, CHIP).astype(BF16), block, (0, 0))
        weight = gates[where, way][:E_WIN]
        coarse = weight.astype(BF16).astype(F32)
        fine = weight - coarse
        coarse = (table_all * coarse[:, None, :]).reshape(E_WIN * SLOT, CHIP).astype(BF16)
        fine = (table_all * fine[:, None, :]).reshape(E_WIN * SLOT, CHIP).astype(BF16)
        return contract(coarse, block, (0, 0)) + contract(fine, block, (0, 0))

    def return3(way):
        for j in (1, 3, 2):
            arrive(ids[way, "rb", 1, j], ret_b.at[way, oy, x_at(4 - j)], x_dev(4 - j))
        mix_out[way] = mixed(way, 1, ret_b[way, oy]).astype(BF16)
        ids[way, "uy"] = send(mix_out.at[way], mix_in.at[way], y_dev)[0]

    def return4(way):
        t = FWD if way == 0 else COT
        for j in (1, 3, 2):
            arrive(ids[way, "rb", 0, j], ret_b.at[way, yh, x_at(4 - j)], x_dev(4 - j))
        total = tok[t, :, QUART:].astype(F32) + mixed(way, 0, ret_b[way, yh])
        arrive(ids[way, "uy"], mix_in.at[way], y_dev)
        fin[way, :, QUART:] = (total + mix_in[way].astype(F32)).astype(BF16)
        for j in (1, 3, 2):
            arrive(ids[way, "ra", j], ret_a.at[way, x_at(4 - j)], x_dev(4 - j))
        fin[way, :, :QUART] = (tok[t, :, :QUART].astype(F32) + mixed(way, 0, ret_a[way])).astype(BF16)
        out = (nxt, gin)[way]
        ids[way, "out"] = send(fin.at[way, lines(oc), :], out.at[:, half(c)], core_dev)[0]
        ids[way, "mine"] = local(fin.at[way, lines(c), :], out.at[:, half(c)])

    def weight_grads():
        step = 512

        def one(k, carry):
            place = pl.ds(pl.multiple_of(k * step, step), step)
            lhs = rows[SAVED, :, :, :, place].reshape(2 * E_WIN * SLOT, step)
            both = contract(lhs, pre_s[...].reshape(2 * E_WIN * SLOT, 2 * HID), (0, 0))
            gate_o[place, :] = both[:, :HID]
            up_o[place, :] = both[:, HID:]
            rhs = rows[COT, :, :, :, place].reshape(2 * E_WIN * SLOT, step)
            down_o[:, place] = contract(hid2_s[...].reshape(2 * E_WIN * SLOT, HID), rhs, (0, 0))
            return carry

        lax.fori_loop(0, D // step, one, 0)

    arrive(i_r1, rts.at[oc], core_dev)
    table(0, 1)
    own_half.wait()
    arrive(i_saved, tok.at[SAVED, lines(oc), :], core_dev)
    stage1(SAVED)
    arrive(i_r2, rts.at[2 + c], y_dev)
    arrive(i_r3, rts.at[2 + oc], diag_dev)
    table(1, 1)
    table(0, 0)
    table(1, 0)
    stage2(SAVED)
    for dc in (0, 1):
        arrive(i_back[dc], tok.at[COT, lines(lax.rem(c + dc, 2)), :], sec_dev(1, dc))
    stage1(COT)
    for dc in (0, 1):
        arrive(i_carry[dc], tok.at[FWD, lines(lax.rem(c + dc, 2)), :], sec_dev(-1, dc))
    stage1(FWD)
    for copy in weights:
        copy.wait()
    stage3(SAVED)
    stage4(SAVED)
    before(oy)
    stage2(COT)
    before(yh)
    stage2(FWD)
    stage3(COT)
    stage4(COT)
    backward(oy)
    backward(yh)
    return1(1)
    stage3(FWD)
    stage4(FWD)
    for key in ("c0", "c1", "c2"):
        sent(ids[FWD, key][1])
    for j in range(4):
        sent(ids[FWD, "ya", j][1])
    forward(oy)
    forward(yh)
    return1(0)
    weight_grads()
    return2(1)
    return3(1)
    return3(0)
    return2(0)
    return4(1)
    return4(0)
    for way, out in ((0, nxt), (1, gin)):
        arrive(ids[way, "out"], out.at[:, half(oc)], core_dev)
        ids[way, "mine"].wait()
    for copy in list(pending):
        copy.wait_send()


def write_out(*refs):
    ins, outs, sem = refs[:5], refs[5:10], refs[10]
    copies = [pltpu.make_async_copy(a, b, sem.at[i]) for i, (a, b) in enumerate(zip(ins, outs))]
    for copy in copies:
        copy.start()
    for copy in copies:
        copy.wait()


def body(carried, saved_rows, returned, fwd_ids, fwd_gates, bwd_ids, bwd_gates, gate_w, up_w, down_w):
    routes = [numbers[0].T for numbers in (fwd_ids, fwd_gates, bwd_ids, bwd_gates)]
    whole = pl.BlockSpec(memory_space=pl.ANY)
    group_rows = E_WIN * SLOT
    scratch = [
        pltpu.VMEM((3, CHIP, HALF), BF16),
        pltpu.VMEM((3, CHIP, QUART), BF16),
        pltpu.VMEM((3, 3, SLOT, QUART), BF16),
        pltpu.VMEM((3, 3, 2, SLOT, QUART), BF16),
        pltpu.VMEM((3, 2, E_WIN, SLOT, D), BF16),
        pltpu.VMEM((D, HID), BF16),
        pltpu.VMEM((D, HID), BF16),
        pltpu.VMEM((HID, D), BF16),
        pltpu.VMEM((8, TOK), F32),
        pltpu.VMEM((4, 8, TOK), F32),
        pltpu.VMEM((2, 2, E_WIN, SLOT, CHIP), BF16),
        pltpu.VMEM((2, 2, 8, CHIP), F32),
        pltpu.VMEM((2, E_WIN, SLOT, HALF), BF16),
        pltpu.VMEM((2, E_WIN, SLOT, HALF), BF16),
        pltpu.VMEM((2, 2, E_WIN, SLOT, HALF), BF16),
        pltpu.VMEM((2, E_WIN, SLOT, QUART), BF16),
        pltpu.VMEM((2, E_WIN, SLOT, QUART), BF16),
        pltpu.VMEM((2, 2, E_WIN, SLOT, QUART), BF16),
        pltpu.VMEM((2, CHIP, QUART), BF16),
        pltpu.VMEM((2, CHIP, QUART), BF16),
        pltpu.VMEM((2, CHIP, HALF), BF16),
        pltpu.VMEM((2, group_rows, HID), F32),
        pltpu.VMEM((2, group_rows, HID), F32),
        pltpu.VMEM((2, group_rows, HID), BF16),
        pltpu.VMEM((2, group_rows, 2 * HID), BF16),
        pltpu.SemaphoreType.DMA((N_COPY,)),
        pltpu.SemaphoreType.DMA((N_COPY,)),
        pltpu.SemaphoreType.DMA((16,)),
    ]
    rows_all = 2 * group_rows
    vmem = pl.BlockSpec(memory_space=pltpu.VMEM)
    results = [((TOK, D), BF16)] * 2 + [((D, HID), F32)] * 2 + [((HID, D), F32)]
    outs = pl.pallas_call(
        kernel,
        name="relay_tick",
        out_shape=tuple(pltpu.VMEM(shape, dtype) for shape, dtype in results),
        in_specs=[whole] * 3 + [vmem] * 4 + [whole] * 3,
        out_specs=(vmem,) * 5,
        scratch_shapes=scratch,
        compiler_params=pltpu.CompilerParams(collective_id=0, has_side_effects=True, vmem_limit_bytes=53 * 2**20),
        cost_estimate=pl.CostEstimate(flops=2 * rows_all * D * 2816, bytes_accessed=12 * 2**20, transcendentals=2 * rows_all * HID),
    )(carried[0], saved_rows[0], returned[0], *routes, gate_w[0], up_w[0], down_w[0])
    outs = pl.pallas_call(
        write_out,
        name="write_out",
        out_shape=tuple(jax.ShapeDtypeStruct(shape, dtype) for shape, dtype in results),
        in_specs=[vmem] * 5,
        out_specs=(whole,) * 5,
        scratch_shapes=[pltpu.SemaphoreType.DMA((5,))],
        compiler_params=pltpu.CompilerParams(vmem_limit_bytes=2**20),
    )(*outs)
    return tuple(out[None] for out in outs)


def solution(mesh):
    tokens = P("section", "expert", None)
    columns = P("section", None, "expert")
    return jax.shard_map(
        body,
        mesh=mesh,
        in_specs=(tokens,) * 7 + (columns, columns, tokens),
        out_specs=(tokens, tokens, columns, columns, tokens),
        check_vma=False,
    )
```

```python
import jax
import jax.numpy as jnp
from jax import lax
from jax.experimental import pallas as pl
from jax.experimental.pallas import tpu as pltpu
from jax.sharding import PartitionSpec as P

E_WIN = 4
TOK = 128
CHIP = 2 * TOK
SLOT = 144
D = 2048
HALF = D // 2
QUART = D // 4
HID = 256
SAVED, FWD, COT = 0, 1, 2
N_COPY = 79
MESH = pl.DeviceIdType.MESH
F32 = jnp.float32
BF16 = jnp.bfloat16


def contract(a, b, dims):
    return lax.dot_general(a, b, ((dims[:1], dims[1:]), ((), ())), preferred_element_type=F32)


def kernel(
    carried, saved, returned, fwd_ids, fwd_gates, bwd_ids, bwd_gates, gate_h, up_h, down_h,
    nxt, gin, gate_o, up_o, down_o,
    tok, toky, pack_a, pack_b, rows, gate, up, down, routes, rts, pick, gates,
    keep_b, part_b, sum_in, ret_y, ret_a, ret_b, mix_out, mix_in, fin,
    swish_s, slope_s, hid2_s, pre_s, ss, rs, ls,
):
    s, r = lax.axis_index("section"), lax.axis_index("expert")
    x, yh, c = r // 4, (r // 2) % 2, r % 2
    oy, oc = 1 - yh, 1 - c
    core_dev = (s, x * 4 + yh * 2 + oc)
    y_dev = (s, x * 4 + oy * 2 + c)
    diag_dev = (s, x * 4 + oy * 2 + oc)

    def x_at(j):
        return lax.rem(x + j, 4)

    def x_dev(j):
        return (s, x_at(j) * 4 + yh * 2 + c)

    def sec_dev(step, dc):
        return (lax.rem(s + step + 16, 16), x * 4 + yh * 2 + lax.rem(c + dc, 2))

    count = [0]
    locals_ = [0]
    pending = []

    def send(src, dst, dev):
        i = count[0]
        count[0] += 1
        copy = pltpu.make_async_remote_copy(
            src_ref=src, dst_ref=dst, send_sem=ss.at[i], recv_sem=rs.at[i], device_id=dev, device_id_type=MESH
        )
        copy.start()
        pending.append(copy)
        return i, copy

    def arrive(i, land, dev):
        pltpu.make_async_remote_copy(
            src_ref=land, dst_ref=land, send_sem=ss.at[i], recv_sem=rs.at[i], device_id=dev, device_id_type=MESH
        ).wait_recv()

    def sent(copy):
        copy.wait_send()
        pending[:] = [other for other in pending if other is not copy]

    def local(src, dst):
        copy = pltpu.make_async_copy(src, dst, ls.at[locals_[0]])
        locals_[0] += 1
        copy.start()
        return copy

    def cols(core, quarter):
        return pl.ds(pl.multiple_of(core * HALF + quarter * QUART, QUART), QUART)

    def half(core):
        return pl.ds(pl.multiple_of(core * HALF, HALF), HALF)

    def lines(core):
        return pl.ds(pl.multiple_of(core * TOK, TOK), TOK)

    barrier = pltpu.get_barrier_semaphore()
    greeted = [core_dev, y_dev, diag_dev, x_dev(1), x_dev(2), x_dev(3), sec_dev(1, 0), sec_dev(1, 1), sec_dev(-1, 0), sec_dev(-1, 1)]
    own_half = local(saved.at[:, half(c)], tok.at[SAVED, lines(c), :])
    weights = [local(gate_h, gate), local(up_h, up), local(down_h, down)]
    for row, numbers in enumerate((fwd_ids, fwd_gates, bwd_ids, bwd_gates)):
        routes[2 * row : 2 * row + 2, :] = numbers[...].astype(F32)
    for dev in greeted:
        pl.semaphore_signal(barrier, inc=1, device_id=dev, device_id_type=MESH)
    pl.semaphore_wait(barrier, len(greeted))
    i_r1, _ = send(routes, rts.at[c], core_dev)
    i_r2, _ = send(routes, rts.at[2 + c], y_dev)
    i_r3, _ = send(routes, rts.at[2 + c], diag_dev)
    i_saved, _ = send(saved.at[:, half(oc)], tok.at[SAVED, lines(c), :], core_dev)
    i_b1 = [
        send(saved.at[:, cols(c, 1)], toky.at[SAVED, lines(c), :], y_dev)[0],
        send(saved.at[:, cols(oc, 1)], toky.at[SAVED, lines(c), :], diag_dev)[0],
    ]
    i_back = [send(returned.at[:, half(lax.rem(c + dc, 2))], tok.at[COT, lines(c), :], sec_dev(-1, dc))[0] for dc in (0, 1)]
    i_carry = [send(carried.at[:, half(lax.rem(c + dc, 2))], tok.at[FWD, lines(c), :], sec_dev(1, dc))[0] for dc in (0, 1)]
    rts[pl.ds(c, 1)] = routes[...][None]

    expert_of = lax.broadcasted_iota(jnp.int32, (8, CHIP), 0).astype(F32)
    slot_of = lax.broadcasted_iota(jnp.int32, (SLOT, CHIP), 0).astype(F32)
    earlier = (
        lax.broadcasted_iota(jnp.int32, (CHIP, CHIP), 0) < lax.broadcasted_iota(jnp.int32, (CHIP, CHIP), 1)
    ).astype(F32).astype(BF16)

    def table(where, way):
        listed = jnp.concatenate([rts[2 * where], rts[2 * where + 1]], axis=1)
        b = 4 * way
        first, second = listed[b : b + 1] == expert_of, listed[b + 1 : b + 2] == expert_of
        chosen = jnp.logical_or(first, second)
        gates[where, way] = jnp.where(first, listed[b + 2 : b + 3], jnp.where(second, listed[b + 3 : b + 4], 0.0))
        rank = jnp.dot(chosen.astype(F32).astype(BF16), earlier, preferred_element_type=F32)
        rank = jnp.where(chosen, rank, -1.0)
        for e in range(E_WIN):
            pick[where, way, e] = (slot_of == rank[e : e + 1]).astype(F32).astype(BF16)

    def picked(what, where, e, tokens):
        way = 0 if what == FWD else 1
        table_e = pick[where, way, e]
        block = jnp.dot(table_e, tokens, preferred_element_type=F32)
        if what == COT:
            gate_e = gates[where, way, pl.ds(e, 1), :]
            block = block * jnp.sum(table_e.astype(F32) * gate_e, axis=1, keepdims=True)
        return block.astype(BF16)

    ids = {}

    def stage1(t):
        if t != SAVED:
            ids[t, "b1"] = send(tok.at[t, :, pl.ds(QUART, QUART)], toky.at[t], y_dev)[0]
        for j in (2, 1, 3, 0):
            block = picked(t, 0, x_at(j), tok[t, :, :QUART])
            if j:
                pack_a[t, j - 1] = block
                ids[t, "xa", j] = send(pack_a.at[t, j - 1], rows.at[t, yh, x, :, cols(c, 0)], x_dev(j))[0]
            else:
                rows[t, yh, x, :, cols(c, 0)] = block

    def stage2(t):
        if t == SAVED:
            arrive(i_b1[0], toky.at[t, lines(c), :], y_dev)
            arrive(i_b1[1], toky.at[t, lines(oc), :], diag_dev)
        else:
            arrive(ids[t, "b1"], toky.at[t], y_dev)
        for j in (2, 1, 3, 0):
            for where, hh in ((0, yh), (1, oy)):
                tokens = tok[t, :, QUART:] if where == 0 else toky[t]
                block = picked(t, where, x_at(j), tokens)
                if j:
                    pack_b[t, j - 1, hh] = block
                else:
                    rows[t, hh, x, :, cols(c, 1)] = block
            if j:
                ids[t, "xb", j] = send(pack_b.at[t, j - 1], rows.at[t, :, x, :, cols(c, 1)], x_dev(j))[0]
        for j in (0, 1, 3, 2):
            place = rows.at[t, yh, x_at(4 - j), :, cols(c, 0)]
            if j:
                arrive(ids[t, "xa", j], place, x_dev(4 - j))
            ids[t, "ya", j] = send(place, place, y_dev)
        place = rows.at[t, yh, :, :, cols(c, 0)]
        ids[t, "c0"] = send(place, place, core_dev)

    def stage3(t):
        for j in (0, 1, 3, 2):
            arrive(ids[t, "ya", j][0], rows.at[t, oy, x_at(4 - j), :, cols(c, 0)], y_dev)
        place = rows.at[t, oy, :, :, cols(c, 0)]
        ids[t, "c1"] = send(place, place, core_dev)
        for j in (1, 3, 2):
            arrive(ids[t, "xb", j], rows.at[t, :, x_at(4 - j), :, cols(c, 1)], x_dev(4 - j))
        place = rows.at[t, :, :, :, cols(c, 1)]
        ids[t, "c2"] = send(place, place, core_dev)

    def stage4(t):
        arrive(ids[t, "c0"][0], rows.at[t, yh, :, :, cols(oc, 0)], core_dev)
        arrive(ids[t, "c1"][0], rows.at[t, oy, :, :, cols(oc, 0)], core_dev)
        arrive(ids[t, "c2"][0], rows.at[t, :, :, :, cols(oc, 1)], core_dev)

    def group(t, hh):
        return rows[t, hh].reshape(E_WIN * SLOT, D)

    keep = (rows.at[FWD, :, :, :, pl.ds(0, HALF)], keep_b)
    part = (rows.at[FWD, :, :, :, pl.ds(HALF, HALF)], part_b)

    def share(way, hh):
        ids[way, "cs", hh is yh] = send(part[way].at[hh], sum_in.at[way, hh], core_dev)[0]

    def forward(hh):
        token_rows = group(FWD, hh)
        pre_gate = jnp.dot(token_rows, gate[...], preferred_element_type=F32)
        pre_up = jnp.dot(token_rows, up[...], preferred_element_type=F32)
        hidden = (pre_gate * jax.nn.sigmoid(pre_gate) * pre_up).astype(BF16)
        for buffer, core in ((part[0], oc), (keep[0], c)):
            out = jnp.dot(hidden, down[:, half(core)], preferred_element_type=F32)
            buffer[hh] = out.astype(BF16).reshape(E_WIN, SLOT, HALF)
            if core is oc:
                share(0, hh)

    def before(hh):
        token_rows = group(SAVED, hh)
        pre_gate = jnp.dot(token_rows, gate[...], preferred_element_type=F32)
        pre_up = jnp.dot(token_rows, up[...], preferred_element_type=F32)
        sig = jax.nn.sigmoid(pre_gate)
        swish = pre_gate * sig
        swish_s[hh] = swish
        slope_s[hh] = pre_up * sig * (1.0 + pre_gate * (1.0 - sig))
        hid2_s[hh] = (swish * pre_up).astype(BF16)

    def backward(hh):
        grad_hidden = contract(group(COT, hh), down[...], (1, 1))
        grad_gate = (grad_hidden * slope_s[hh]).astype(BF16)
        grad_up = (grad_hidden * swish_s[hh]).astype(BF16)
        pre_s[hh, :, :HID] = grad_gate
        pre_s[hh, :, HID:] = grad_up
        for buffer, core in ((part[1], oc), (keep[1], c)):
            out = contract(grad_gate, gate[half(core), :], (1, 1)) + contract(grad_up, up[half(core), :], (1, 1))
            buffer[hh] = out.astype(BF16).reshape(E_WIN, SLOT, HALF)
            if core is oc:
                share(1, hh)

    def add_core(way, hh):
        arrive(ids[way, "cs", hh is yh], sum_in.at[way, hh], core_dev)
        keep[way][hh] = (keep[way][hh].astype(F32) + sum_in[way, hh].astype(F32)).astype(BF16)

    def return1(way):
        for where, hh in ((1, oy), (0, yh)):
            add_core(way, hh)
            if where:
                ids[way, "ry"] = send(keep[way].at[oy, :, :, pl.ds(0, QUART)], ret_y.at[way], y_dev)[0]
            for j in (2, 1, 3):
                ids[way, "rb", where, j] = send(
                    keep[way].at[hh, x_at(j), :, pl.ds(QUART, QUART)], ret_b.at[way, hh, x], x_dev(j)
                )[0]
            ret_b[way, hh, x] = keep[way][hh, x, :, QUART:]

    def return2(way):
        arrive(ids[way, "ry"], ret_y.at[way], y_dev)
        both = keep[way][yh, :, :, :QUART].astype(F32) + ret_y[way].astype(F32)
        keep[way][yh, :, :, :QUART] = both.astype(BF16)
        for j in (2, 1, 3):
            ids[way, "ra", j] = send(keep[way].at[yh, x_at(j), :, pl.ds(0, QUART)], ret_a.at[way, x], x_dev(j))[0]
        ret_a[way, x] = keep[way][yh, x, :, :QUART]

    def mixed(way, where, e, block):
        table_e = pick[where, way, e]
        if way == 1:
            return contract(table_e, block, (0, 0))
        weight = gates[where, way, pl.ds(e, 1), :]
        coarse = weight.astype(BF16).astype(F32)
        wide = table_e.astype(F32)
        parts = [(wide * part_of).astype(BF16) for part_of in (coarse, weight - coarse)]
        return contract(parts[0], block, (0, 0)) + contract(parts[1], block, (0, 0))

    def return3(way):
        total = mixed(way, 1, x, ret_b[way, oy, x])
        for j in (1, 3, 2):
            e = x_at(4 - j)
            arrive(ids[way, "rb", 1, j], ret_b.at[way, oy, e], x_dev(4 - j))
            total = total + mixed(way, 1, e, ret_b[way, oy, e])
        mix_out[way] = total.astype(BF16)
        ids[way, "uy"] = send(mix_out.at[way], mix_in.at[way], y_dev)[0]

    def return4(way):
        t = FWD if way == 0 else COT
        total = tok[t, :, QUART:].astype(F32) + mixed(way, 0, x, ret_b[way, yh, x])
        for j in (1, 3, 2):
            e = x_at(4 - j)
            arrive(ids[way, "rb", 0, j], ret_b.at[way, yh, e], x_dev(4 - j))
            total = total + mixed(way, 0, e, ret_b[way, yh, e])
        arrive(ids[way, "uy"], mix_in.at[way], y_dev)
        fin[way, :, QUART:] = (total + mix_in[way].astype(F32)).astype(BF16)
        total = tok[t, :, :QUART].astype(F32) + mixed(way, 0, x, ret_a[way, x])
        for j in (1, 3, 2):
            e = x_at(4 - j)
            arrive(ids[way, "ra", j], ret_a.at[way, e], x_dev(4 - j))
            total = total + mixed(way, 0, e, ret_a[way, e])
        fin[way, :, :QUART] = total.astype(BF16)
        out = (nxt, gin)[way]
        ids[way, "out"] = send(fin.at[way, lines(oc), :], out.at[:, half(c)], core_dev)[0]
        ids[way, "mine"] = local(fin.at[way, lines(c), :], out.at[:, half(c)])

    def weight_grads():
        step = 512

        def one(k, carry):
            place = pl.ds(pl.multiple_of(k * step, step), step)
            lhs = rows[SAVED, :, :, :, place].reshape(2 * E_WIN * SLOT, step)
            both = contract(lhs, pre_s[...].reshape(2 * E_WIN * SLOT, 2 * HID), (0, 0))
            gate_o[place, :] = both[:, :HID]
            up_o[place, :] = both[:, HID:]
            rhs = rows[COT, :, :, :, place].reshape(2 * E_WIN * SLOT, step)
            down_o[:, place] = contract(hid2_s[...].reshape(2 * E_WIN * SLOT, HID), rhs, (0, 0))
            return carry

        lax.fori_loop(0, D // step, one, 0)

    arrive(i_r1, rts.at[oc], core_dev)
    table(0, 1)
    own_half.wait()
    arrive(i_saved, tok.at[SAVED, lines(oc), :], core_dev)
    stage1(SAVED)
    arrive(i_r2, rts.at[2 + c], y_dev)
    arrive(i_r3, rts.at[2 + oc], diag_dev)
    table(1, 1)
    table(0, 0)
    table(1, 0)
    stage2(SAVED)
    for dc in (0, 1):
        arrive(i_back[dc], tok.at[COT, lines(lax.rem(c + dc, 2)), :], sec_dev(1, dc))
    stage1(COT)
    for dc in (0, 1):
        arrive(i_carry[dc], tok.at[FWD, lines(lax.rem(c + dc, 2)), :], sec_dev(-1, dc))
    stage1(FWD)
    for copy in weights:
        copy.wait()
    stage2(COT)
    stage3(SAVED)
    stage4(SAVED)
    before(oy)
    stage2(FWD)
    before(yh)
    stage3(COT)
    stage4(COT)
    backward(oy)
    backward(yh)
    return1(1)
    stage3(FWD)
    stage4(FWD)
    for key in ("c0", "c1", "c2"):
        sent(ids[FWD, key][1])
    for j in range(4):
        sent(ids[FWD, "ya", j][1])
    forward(oy)
    forward(yh)
    return1(0)
    weight_grads()
    return2(1)
    return3(1)
    return3(0)
    return2(0)
    return4(1)
    return4(0)
    for way, out in ((0, nxt), (1, gin)):
        arrive(ids[way, "out"], out.at[:, half(oc)], core_dev)
        ids[way, "mine"].wait()
    for copy in list(pending):
        copy.wait_send()


def write_out(*refs):
    ins, outs, sem = refs[:5], refs[5:10], refs[10]
    copies = [pltpu.make_async_copy(a, b, sem.at[i]) for i, (a, b) in enumerate(zip(ins, outs))]
    for copy in copies:
        copy.start()
    for copy in copies:
        copy.wait()


def body(carried, saved_rows, returned, fwd_ids, fwd_gates, bwd_ids, bwd_gates, gate_w, up_w, down_w):
    routes = [numbers[0].T for numbers in (fwd_ids, fwd_gates, bwd_ids, bwd_gates)]
    whole = pl.BlockSpec(memory_space=pl.ANY)
    group_rows = E_WIN * SLOT
    scratch = [
        pltpu.VMEM((3, CHIP, HALF), BF16),
        pltpu.VMEM((3, CHIP, QUART), BF16),
        pltpu.VMEM((3, 3, SLOT, QUART), BF16),
        pltpu.VMEM((3, 3, 2, SLOT, QUART), BF16),
        pltpu.VMEM((3, 2, E_WIN, SLOT, D), BF16),
        pltpu.VMEM((D, HID), BF16),
        pltpu.VMEM((D, HID), BF16),
        pltpu.VMEM((HID, D), BF16),
        pltpu.VMEM((8, TOK), F32),
        pltpu.VMEM((4, 8, TOK), F32),
        pltpu.VMEM((2, 2, E_WIN, SLOT, CHIP), BF16),
        pltpu.VMEM((2, 2, 8, CHIP), F32),
        pltpu.VMEM((2, E_WIN, SLOT, HALF), BF16),
        pltpu.VMEM((2, E_WIN, SLOT, HALF), BF16),
        pltpu.VMEM((2, 2, E_WIN, SLOT, HALF), BF16),
        pltpu.VMEM((2, E_WIN, SLOT, QUART), BF16),
        pltpu.VMEM((2, E_WIN, SLOT, QUART), BF16),
        pltpu.VMEM((2, 2, E_WIN, SLOT, QUART), BF16),
        pltpu.VMEM((2, CHIP, QUART), BF16),
        pltpu.VMEM((2, CHIP, QUART), BF16),
        pltpu.VMEM((2, CHIP, HALF), BF16),
        pltpu.VMEM((2, group_rows, HID), F32),
        pltpu.VMEM((2, group_rows, HID), F32),
        pltpu.VMEM((2, group_rows, HID), BF16),
        pltpu.VMEM((2, group_rows, 2 * HID), BF16),
        pltpu.SemaphoreType.DMA((N_COPY,)),
        pltpu.SemaphoreType.DMA((N_COPY,)),
        pltpu.SemaphoreType.DMA((9,)),
    ]
    rows_all = 2 * group_rows
    vmem = pl.BlockSpec(memory_space=pltpu.VMEM)
    results = [((TOK, D), BF16)] * 2 + [((D, HID), F32)] * 2 + [((HID, D), F32)]
    outs = pl.pallas_call(
        kernel,
        name="relay_tick",
        out_shape=tuple(pltpu.VMEM(shape, dtype) for shape, dtype in results),
        in_specs=[whole] * 3 + [vmem] * 4 + [whole] * 3,
        out_specs=(vmem,) * 5,
        scratch_shapes=scratch,
        compiler_params=pltpu.CompilerParams(collective_id=0, has_side_effects=True, vmem_limit_bytes=53 * 2**20),
        cost_estimate=pl.CostEstimate(flops=2 * rows_all * D * 2816, bytes_accessed=12 * 2**20, transcendentals=2 * rows_all * HID),
    )(carried[0], saved_rows[0], returned[0], *routes, gate_w[0], up_w[0], down_w[0])
    outs = pl.pallas_call(
        write_out,
        name="write_out",
        out_shape=tuple(jax.ShapeDtypeStruct(shape, dtype) for shape, dtype in results),
        in_specs=[vmem] * 5,
        out_specs=(whole,) * 5,
        scratch_shapes=[pltpu.SemaphoreType.DMA((5,))],
        compiler_params=pltpu.CompilerParams(vmem_limit_bytes=2**20),
    )(*outs)
    return tuple(out[None] for out in outs)


def solution(mesh):
    tokens = P("section", "expert", None)
    columns = P("section", None, "expert")
    return jax.shard_map(
        body,
        mesh=mesh,
        in_specs=(tokens,) * 7 + (columns, columns, tokens),
        out_specs=(tokens, tokens, columns, columns, tokens),
        check_vma=False,
    )
```

```python
import jax
import jax.numpy as jnp
from jax import lax
from jax.experimental import pallas as pl
from jax.experimental.pallas import tpu as pltpu
from jax.sharding import PartitionSpec as P

E_WIN = 4
TOK = 128
CHIP = 2 * TOK
SLOT = 144
D = 2048
HALF = D // 2
QUART = D // 4
HID = 256
SAVED, FWD, COT = 0, 1, 2
A_WIDE = {SAVED: QUART, FWD: 384, COT: QUART}
B_MOST = HALF - 384
N_COPY = 79
MESH = pl.DeviceIdType.MESH
F32 = jnp.float32
BF16 = jnp.bfloat16


def contract(a, b, dims):
    return lax.dot_general(a, b, ((dims[:1], dims[1:]), ((), ())), preferred_element_type=F32)


def kernel(
    carried, saved, returned, fwd_ids, fwd_gates, bwd_ids, bwd_gates, gate_h, up_h, down_h,
    nxt, gin, gate_o, up_o, down_o,
    tok, toky, pack_a, pack_b, rows, gate, up, down, routes, rts, pick, gates,
    keep_b, part_b, sum_in, ret_y, ret_a, ret_b, mix_out, mix_in, fin,
    swish_s, slope_s, hid2_s, pre_s, ss, rs, ls,
):
    s, r = lax.axis_index("section"), lax.axis_index("expert")
    x, yh, c = r // 4, (r // 2) % 2, r % 2
    oy, oc = 1 - yh, 1 - c
    core_dev = (s, x * 4 + yh * 2 + oc)
    y_dev = (s, x * 4 + oy * 2 + c)
    diag_dev = (s, x * 4 + oy * 2 + oc)

    def x_at(j):
        return lax.rem(x + j, 4)

    def x_dev(j):
        return (s, x_at(j) * 4 + yh * 2 + c)

    def sec_dev(step, dc):
        return (lax.rem(s + step + 16, 16), x * 4 + yh * 2 + lax.rem(c + dc, 2))

    count = [0]
    locals_ = [0]
    pending = []

    def send(src, dst, dev):
        i = count[0]
        count[0] += 1
        copy = pltpu.make_async_remote_copy(
            src_ref=src, dst_ref=dst, send_sem=ss.at[i], recv_sem=rs.at[i], device_id=dev, device_id_type=MESH
        )
        copy.start()
        pending.append(copy)
        return i, copy

    def arrive(i, land, dev):
        pltpu.make_async_remote_copy(
            src_ref=land, dst_ref=land, send_sem=ss.at[i], recv_sem=rs.at[i], device_id=dev, device_id_type=MESH
        ).wait_recv()

    def sent(copy):
        copy.wait_send()
        pending[:] = [other for other in pending if other is not copy]

    def local(src, dst):
        copy = pltpu.make_async_copy(src, dst, ls.at[locals_[0]])
        locals_[0] += 1
        copy.start()
        return copy

    def width(t, part_of):
        return HALF - A_WIDE[t] if part_of else A_WIDE[t]

    def cols(t, core, part_of):
        return pl.ds(pl.multiple_of(core * HALF + part_of * A_WIDE[t], 128), width(t, part_of))

    def half(core):
        return pl.ds(pl.multiple_of(core * HALF, HALF), HALF)

    def lines(core):
        return pl.ds(pl.multiple_of(core * TOK, TOK), TOK)

    barrier = pltpu.get_barrier_semaphore()
    greeted = [core_dev, y_dev, diag_dev, x_dev(1), x_dev(2), x_dev(3), sec_dev(1, 0), sec_dev(1, 1), sec_dev(-1, 0), sec_dev(-1, 1)]
    own_half = local(saved.at[:, half(c)], tok.at[SAVED, lines(c), :])
    weights = [local(gate_h, gate), local(up_h, up), local(down_h, down)]
    for row, numbers in enumerate((fwd_ids, fwd_gates, bwd_ids, bwd_gates)):
        routes[2 * row : 2 * row + 2, :] = numbers[...].astype(F32)
    for dev in greeted:
        pl.semaphore_signal(barrier, inc=1, device_id=dev, device_id_type=MESH)
    pl.semaphore_wait(barrier, len(greeted))
    i_r1, _ = send(routes, rts.at[c], core_dev)
    i_r2, _ = send(routes, rts.at[2 + c], y_dev)
    i_r3, _ = send(routes, rts.at[2 + c], diag_dev)
    i_saved, _ = send(saved.at[:, half(oc)], tok.at[SAVED, lines(c), :], core_dev)
    i_b1 = [
        send(saved.at[:, cols(SAVED, c, 1)], toky.at[SAVED, lines(c), pl.ds(0, width(SAVED, 1))], y_dev)[0],
        send(saved.at[:, cols(SAVED, oc, 1)], toky.at[SAVED, lines(c), pl.ds(0, width(SAVED, 1))], diag_dev)[0],
    ]
    i_back = [send(returned.at[:, half(lax.rem(c + dc, 2))], tok.at[COT, lines(c), :], sec_dev(-1, dc))[0] for dc in (0, 1)]
    i_carry = [send(carried.at[:, half(lax.rem(c + dc, 2))], tok.at[FWD, lines(c), :], sec_dev(1, dc))[0] for dc in (0, 1)]
    rts[pl.ds(c, 1)] = routes[...][None]

    expert_of = lax.broadcasted_iota(jnp.int32, (8, CHIP), 0).astype(F32)
    slot_of = lax.broadcasted_iota(jnp.int32, (SLOT, CHIP), 0).astype(F32)
    earlier = (
        lax.broadcasted_iota(jnp.int32, (CHIP, CHIP), 0) < lax.broadcasted_iota(jnp.int32, (CHIP, CHIP), 1)
    ).astype(F32).astype(BF16)

    def table(where, way):
        listed = jnp.concatenate([rts[2 * where], rts[2 * where + 1]], axis=1)
        b = 4 * way
        first, second = listed[b : b + 1] == expert_of, listed[b + 1 : b + 2] == expert_of
        chosen = jnp.logical_or(first, second)
        gates[where, way] = jnp.where(first, listed[b + 2 : b + 3], jnp.where(second, listed[b + 3 : b + 4], 0.0))
        rank = jnp.dot(chosen.astype(F32).astype(BF16), earlier, preferred_element_type=F32)
        rank = jnp.where(chosen, rank, -1.0)
        for e in range(E_WIN):
            pick[where, way, e] = (slot_of == rank[e : e + 1]).astype(F32).astype(BF16)

    def picked(what, where, e, tokens):
        way = 0 if what == FWD else 1
        table_e = pick[where, way, e]
        block = jnp.dot(table_e, tokens, preferred_element_type=F32)
        if what == COT:
            gate_e = gates[where, way, pl.ds(e, 1), :]
            block = block * jnp.sum(table_e.astype(F32) * gate_e, axis=1, keepdims=True)
        return block.astype(BF16)

    ids = {}

    def stage1(t):
        if t != SAVED:
            ids[t, "b1"] = send(tok.at[t, :, pl.ds(width(t, 0), width(t, 1))], toky.at[t, :, pl.ds(0, width(t, 1))], y_dev)[0]
        for j in (2, 1, 3, 0):
            block = picked(t, 0, x_at(j), tok[t, :, : width(t, 0)])
            if j:
                pack_a[t, j - 1, :, : width(t, 0)] = block
                ids[t, "xa", j] = send(pack_a.at[t, j - 1, :, pl.ds(0, width(t, 0))], rows.at[t, yh, x, :, cols(t, c, 0)], x_dev(j))[0]
            else:
                rows[t, yh, x, :, cols(t, c, 0)] = block

    def stage2(t):
        if t == SAVED:
            arrive(i_b1[0], toky.at[t, lines(c), pl.ds(0, width(t, 1))], y_dev)
            arrive(i_b1[1], toky.at[t, lines(oc), pl.ds(0, width(t, 1))], diag_dev)
        else:
            arrive(ids[t, "b1"], toky.at[t, :, pl.ds(0, width(t, 1))], y_dev)
        for j in (2, 1, 3, 0):
            for where, hh in ((0, yh), (1, oy)):
                tokens = tok[t, :, width(t, 0) :] if where == 0 else toky[t, :, : width(t, 1)]
                block = picked(t, where, x_at(j), tokens)
                if j:
                    pack_b[t, j - 1, hh, :, : width(t, 1)] = block
                else:
                    rows[t, hh, x, :, cols(t, c, 1)] = block
            if j:
                ids[t, "xb", j] = send(pack_b.at[t, j - 1, :, :, pl.ds(0, width(t, 1))], rows.at[t, :, x, :, cols(t, c, 1)], x_dev(j))[0]
        for j in (0, 1, 3, 2):
            place = rows.at[t, yh, x_at(4 - j), :, cols(t, c, 0)]
            if j:
                arrive(ids[t, "xa", j], place, x_dev(4 - j))
            ids[t, "ya", j] = send(place, place, y_dev)
        place = rows.at[t, yh, :, :, cols(t, c, 0)]
        ids[t, "c0"] = send(place, place, core_dev)

    def stage3(t):
        for j in (0, 1, 3, 2):
            arrive(ids[t, "ya", j][0], rows.at[t, oy, x_at(4 - j), :, cols(t, c, 0)], y_dev)
        place = rows.at[t, oy, :, :, cols(t, c, 0)]
        ids[t, "c1"] = send(place, place, core_dev)
        for j in (1, 3, 2):
            arrive(ids[t, "xb", j], rows.at[t, :, x_at(4 - j), :, cols(t, c, 1)], x_dev(4 - j))
        place = rows.at[t, :, :, :, cols(t, c, 1)]
        ids[t, "c2"] = send(place, place, core_dev)

    def stage4(t):
        arrive(ids[t, "c0"][0], rows.at[t, yh, :, :, cols(t, oc, 0)], core_dev)
        arrive(ids[t, "c1"][0], rows.at[t, oy, :, :, cols(t, oc, 0)], core_dev)
        arrive(ids[t, "c2"][0], rows.at[t, :, :, :, cols(t, oc, 1)], core_dev)

    def group(t, hh):
        return rows[t, hh].reshape(E_WIN * SLOT, D)

    keep = (rows.at[FWD, :, :, :, pl.ds(0, HALF)], keep_b)
    part = (rows.at[FWD, :, :, :, pl.ds(HALF, HALF)], part_b)

    def share(way, hh):
        ids[way, "cs", hh is yh] = send(part[way].at[hh], sum_in.at[way, hh], core_dev)[0]

    def forward(hh):
        token_rows = group(FWD, hh)
        pre_gate = jnp.dot(token_rows, gate[...], preferred_element_type=F32)
        pre_up = jnp.dot(token_rows, up[...], preferred_element_type=F32)
        hidden = (pre_gate * jax.nn.sigmoid(pre_gate) * pre_up).astype(BF16)
        for buffer, core in ((part[0], oc), (keep[0], c)):
            out = jnp.dot(hidden, down[:, half(core)], preferred_element_type=F32)
            buffer[hh] = out.astype(BF16).reshape(E_WIN, SLOT, HALF)
            if core is oc:
                share(0, hh)

    def before(hh):
        token_rows = group(SAVED, hh)
        pre_gate = jnp.dot(token_rows, gate[...], preferred_element_type=F32)
        pre_up = jnp.dot(token_rows, up[...], preferred_element_type=F32)
        sig = jax.nn.sigmoid(pre_gate)
        swish = pre_gate * sig
        swish_s[hh] = swish
        slope_s[hh] = pre_up * sig * (1.0 + pre_gate * (1.0 - sig))
        hid2_s[hh] = (swish * pre_up).astype(BF16)

    def backward(hh):
        grad_hidden = contract(group(COT, hh), down[...], (1, 1))
        grad_gate = (grad_hidden * slope_s[hh]).astype(BF16)
        grad_up = (grad_hidden * swish_s[hh]).astype(BF16)
        pre_s[hh, :, :HID] = grad_gate
        pre_s[hh, :, HID:] = grad_up
        for buffer, core in ((part[1], oc), (keep[1], c)):
            out = contract(grad_gate, gate[half(core), :], (1, 1)) + contract(grad_up, up[half(core), :], (1, 1))
            buffer[hh] = out.astype(BF16).reshape(E_WIN, SLOT, HALF)
            if core is oc:
                share(1, hh)

    def add_core(way, hh):
        arrive(ids[way, "cs", hh is yh], sum_in.at[way, hh], core_dev)
        keep[way][hh] = (keep[way][hh].astype(F32) + sum_in[way, hh].astype(F32)).astype(BF16)

    def return1(way):
        for where, hh in ((1, oy), (0, yh)):
            add_core(way, hh)
            if where:
                ids[way, "ry"] = send(keep[way].at[oy, :, :, pl.ds(0, QUART)], ret_y.at[way], y_dev)[0]
            for j in (2, 1, 3):
                ids[way, "rb", where, j] = send(
                    keep[way].at[hh, x_at(j), :, pl.ds(QUART, QUART)], ret_b.at[way, hh, x], x_dev(j)
                )[0]
            ret_b[way, hh, x] = keep[way][hh, x, :, QUART:]

    def return2(way):
        arrive(ids[way, "ry"], ret_y.at[way], y_dev)
        both = keep[way][yh, :, :, :QUART].astype(F32) + ret_y[way].astype(F32)
        keep[way][yh, :, :, :QUART] = both.astype(BF16)
        for j in (2, 1, 3):
            ids[way, "ra", j] = send(keep[way].at[yh, x_at(j), :, pl.ds(0, QUART)], ret_a.at[way, x], x_dev(j))[0]
        ret_a[way, x] = keep[way][yh, x, :, :QUART]

    def mixed(way, where, e, block):
        table_e = pick[where, way, e]
        if way == 1:
            return contract(table_e, block, (0, 0))
        weight = gates[where, way, pl.ds(e, 1), :]
        coarse = weight.astype(BF16).astype(F32)
        wide = table_e.astype(F32)
        parts = [(wide * part_of).astype(BF16) for part_of in (coarse, weight - coarse)]
        return contract(parts[0], block, (0, 0)) + contract(parts[1], block, (0, 0))

    def return3(way):
        total = mixed(way, 1, x, ret_b[way, oy, x])
        for j in (1, 3, 2):
            e = x_at(4 - j)
            arrive(ids[way, "rb", 1, j], ret_b.at[way, oy, e], x_dev(4 - j))
            total = total + mixed(way, 1, e, ret_b[way, oy, e])
        mix_out[way] = total.astype(BF16)
        ids[way, "uy"] = send(mix_out.at[way], mix_in.at[way], y_dev)[0]

    def return4(way):
        t = FWD if way == 0 else COT
        total = tok[t, :, QUART:].astype(F32) + mixed(way, 0, x, ret_b[way, yh, x])
        for j in (1, 3, 2):
            e = x_at(4 - j)
            arrive(ids[way, "rb", 0, j], ret_b.at[way, yh, e], x_dev(4 - j))
            total = total + mixed(way, 0, e, ret_b[way, yh, e])
        arrive(ids[way, "uy"], mix_in.at[way], y_dev)
        fin[way, :, QUART:] = (total + mix_in[way].astype(F32)).astype(BF16)
        total = tok[t, :, :QUART].astype(F32) + mixed(way, 0, x, ret_a[way, x])
        for j in (1, 3, 2):
            e = x_at(4 - j)
            arrive(ids[way, "ra", j], ret_a.at[way, e], x_dev(4 - j))
            total = total + mixed(way, 0, e, ret_a[way, e])
        fin[way, :, :QUART] = total.astype(BF16)
        out = (nxt, gin)[way]
        ids[way, "out"] = send(fin.at[way, lines(oc), :], out.at[:, half(c)], core_dev)[0]
        ids[way, "mine"] = local(fin.at[way, lines(c), :], out.at[:, half(c)])

    def weight_grads():
        step = 512

        def one(k, carry):
            place = pl.ds(pl.multiple_of(k * step, step), step)
            lhs = rows[SAVED, :, :, :, place].reshape(2 * E_WIN * SLOT, step)
            both = contract(lhs, pre_s[...].reshape(2 * E_WIN * SLOT, 2 * HID), (0, 0))
            gate_o[place, :] = both[:, :HID]
            up_o[place, :] = both[:, HID:]
            rhs = rows[COT, :, :, :, place].reshape(2 * E_WIN * SLOT, step)
            down_o[:, place] = contract(hid2_s[...].reshape(2 * E_WIN * SLOT, HID), rhs, (0, 0))
            return carry

        lax.fori_loop(0, D // step, one, 0)

    arrive(i_r1, rts.at[oc], core_dev)
    table(0, 1)
    own_half.wait()
    arrive(i_saved, tok.at[SAVED, lines(oc), :], core_dev)
    stage1(SAVED)
    arrive(i_r2, rts.at[2 + c], y_dev)
    arrive(i_r3, rts.at[2 + oc], diag_dev)
    table(1, 1)
    table(0, 0)
    table(1, 0)
    stage2(SAVED)
    for dc in (0, 1):
        arrive(i_back[dc], tok.at[COT, lines(lax.rem(c + dc, 2)), :], sec_dev(1, dc))
    stage1(COT)
    for dc in (0, 1):
        arrive(i_carry[dc], tok.at[FWD, lines(lax.rem(c + dc, 2)), :], sec_dev(-1, dc))
    stage1(FWD)
    for copy in weights:
        copy.wait()
    stage2(COT)
    stage3(SAVED)
    stage4(SAVED)
    before(oy)
    stage2(FWD)
    before(yh)
    stage3(COT)
    stage4(COT)
    backward(oy)
    backward(yh)
    return1(1)
    stage3(FWD)
    stage4(FWD)
    for key in ("c0", "c1", "c2"):
        sent(ids[FWD, key][1])
    for j in range(4):
        sent(ids[FWD, "ya", j][1])
    forward(oy)
    forward(yh)
    return1(0)
    weight_grads()
    return2(1)
    return3(1)
    return3(0)
    return2(0)
    return4(1)
    return4(0)
    for way, out in ((0, nxt), (1, gin)):
        arrive(ids[way, "out"], out.at[:, half(oc)], core_dev)
        ids[way, "mine"].wait()
    for copy in list(pending):
        copy.wait_send()


def write_out(*refs):
    ins, outs, sem = refs[:5], refs[5:10], refs[10]
    copies = [pltpu.make_async_copy(a, b, sem.at[i]) for i, (a, b) in enumerate(zip(ins, outs))]
    for copy in copies:
        copy.start()
    for copy in copies:
        copy.wait()


def body(carried, saved_rows, returned, fwd_ids, fwd_gates, bwd_ids, bwd_gates, gate_w, up_w, down_w):
    routes = [numbers[0].T for numbers in (fwd_ids, fwd_gates, bwd_ids, bwd_gates)]
    whole = pl.BlockSpec(memory_space=pl.ANY)
    group_rows = E_WIN * SLOT
    scratch = [
        pltpu.VMEM((3, CHIP, HALF), BF16),
        pltpu.VMEM((3, CHIP, B_MOST), BF16),
        pltpu.VMEM((3, 3, SLOT, QUART), BF16),
        pltpu.VMEM((3, 3, 2, SLOT, B_MOST), BF16),
        pltpu.VMEM((3, 2, E_WIN, SLOT, D), BF16),
        pltpu.VMEM((D, HID), BF16),
        pltpu.VMEM((D, HID), BF16),
        pltpu.VMEM((HID, D), BF16),
        pltpu.VMEM((8, TOK), F32),
        pltpu.VMEM((4, 8, TOK), F32),
        pltpu.VMEM((2, 2, E_WIN, SLOT, CHIP), BF16),
        pltpu.VMEM((2, 2, 8, CHIP), F32),
        pltpu.VMEM((2, E_WIN, SLOT, HALF), BF16),
        pltpu.VMEM((2, E_WIN, SLOT, HALF), BF16),
        pltpu.VMEM((2, 2, E_WIN, SLOT, HALF), BF16),
        pltpu.VMEM((2, E_WIN, SLOT, QUART), BF16),
        pltpu.VMEM((2, E_WIN, SLOT, QUART), BF16),
        pltpu.VMEM((2, 2, E_WIN, SLOT, QUART), BF16),
        pltpu.VMEM((2, CHIP, QUART), BF16),
        pltpu.VMEM((2, CHIP, QUART), BF16),
        pltpu.VMEM((2, CHIP, HALF), BF16),
        pltpu.VMEM((2, group_rows, HID), F32),
        pltpu.VMEM((2, group_rows, HID), F32),
        pltpu.VMEM((2, group_rows, HID), BF16),
        pltpu.VMEM((2, group_rows, 2 * HID), BF16),
        pltpu.SemaphoreType.DMA((N_COPY,)),
        pltpu.SemaphoreType.DMA((N_COPY,)),
        pltpu.SemaphoreType.DMA((9,)),
    ]
    rows_all = 2 * group_rows
    vmem = pl.BlockSpec(memory_space=pltpu.VMEM)
    results = [((TOK, D), BF16)] * 2 + [((D, HID), F32)] * 2 + [((HID, D), F32)]
    outs = pl.pallas_call(
        kernel,
        name="relay_tick",
        out_shape=tuple(pltpu.VMEM(shape, dtype) for shape, dtype in results),
        in_specs=[whole] * 3 + [vmem] * 4 + [whole] * 3,
        out_specs=(vmem,) * 5,
        scratch_shapes=scratch,
        compiler_params=pltpu.CompilerParams(collective_id=0, has_side_effects=True, vmem_limit_bytes=53 * 2**20),
        cost_estimate=pl.CostEstimate(flops=2 * rows_all * D * 2816, bytes_accessed=12 * 2**20, transcendentals=2 * rows_all * HID),
    )(carried[0], saved_rows[0], returned[0], *routes, gate_w[0], up_w[0], down_w[0])
    outs = pl.pallas_call(
        write_out,
        name="write_out",
        out_shape=tuple(jax.ShapeDtypeStruct(shape, dtype) for shape, dtype in results),
        in_specs=[vmem] * 5,
        out_specs=(whole,) * 5,
        scratch_shapes=[pltpu.SemaphoreType.DMA((5,))],
        compiler_params=pltpu.CompilerParams(vmem_limit_bytes=2**20),
    )(*outs)
    return tuple(out[None] for out in outs)


def solution(mesh):
    tokens = P("section", "expert", None)
    columns = P("section", None, "expert")
    return jax.shard_map(
        body,
        mesh=mesh,
        in_specs=(tokens,) * 7 + (columns, columns, tokens),
        out_specs=(tokens, tokens, columns, columns, tokens),
        check_vma=False,
    )
```
